32 devices in a mesh: circ: 8 (over z, x), axial: 4 (over y, core).
Axes of the slice: x: 2, y: 2, z: 4, core: 2. Of those that a mesh axis runs over, the one named last changes fastest.
Arguments:
- seal_state: float32 [12, 512, 512], P(None, 'circ', 'axial'), may hold values from -6 to 6
- seal_blocks: bfloat16 [5, 36, 512, 512], P(None, None, 'circ', 'axial'), may hold values from -0.875 to 0.875
- seal_scales: float32 [5, 512, 512], P(None, 'circ', 'axial'), may hold values from 0.3 to 3
- seal_volume: float32 [512, 512], P('circ', 'axial'), may hold values from 0.3 to 3
- cavity_state: float32 [12, 32768], P(None, ('circ', 'axial')), may hold values from -6 to 6
- cavity_blocks: bfloat16 [5, 36, 32768], P(None, None, ('circ', 'axial')), may hold values from -0.875 to 0.875
- cavity_scales: float32 [5, 32768], P(None, ('circ', 'axial')), may hold values from 0.3 to 3
- cavity_links: int32 [4, 32768], P(None, ('circ', 'axial')), may hold values from 0 to 1023
- cavity_volume: float32 [32768], P(('circ', 'axial')), may hold values from 0.3 to 3
- link_owner: int32 [65536, 1], P(('circ', 'axial')), may hold values from 0 to 7; in each aligned block of 2048 rows (0 to 2047, 2048 to 4095, ...) at most 512 rows name the same one
- link_seal: int32 [65536], P(('circ', 'axial')), may hold values from 0 to 8191
- link_cavity: int32 [65536], P(('circ', 'axial')), may hold values from 0 to 1023
- link_blocks: bfloat16 [2, 36, 65536], P(None, None, ('circ', 'axial')), may hold values from -0.875 to 0.875
- link_scales: float32 [2, 65536], P(None, ('circ', 'axial')), may hold values from 0.3 to 3
Outputs:
- seal_residual: float32 [12, 512, 512], P(None, 'circ', 'axial')
- cavity_residual: float32 [12, 32768], P(None, ('circ', 'axial'))
The draws below stay inside these ranges and needn't reach their ends.
Inputs may be any that keep to these rules, and one draw needn't show every extreme that they name: `link_owner`: among the rows of one device, no sector is named by more than 512 rows, and in every draw some device names some sector exactly 512 times.
All inputs are finite; a program needn't handle non-finite values.
Results may differ from the reference program's by a relative error of at most 0.0003.
Values may be sent and summed in bfloat16 or wider, within the bound.
No kernel may reach another device: no remote copies, remote signals or barrier semaphores. Data moves between devices by JAX's collectives and lax.ppermute only.
A program may use at most 64 MiB of HBM per device.

```python
import math
import jax
import jax.numpy as jnp
import numpy as np

CC = 64
CA = 128
CV = 1024
IF_DEV = 2048
CAP = 512
NC = 512
NA = 512
NCAV = 32768
NIF = 65536
N_CIRC = 8
N_AXIAL = 4


def place_ends(result, key, smallest, largest):
    index_at = [jax.random.randint(jax.random.fold_in(key, axis), (), 0, length) for axis, length in enumerate(result.shape)]
    main_axis = result.shape.index(max(result.shape))
    beside = index_at[:main_axis] + [(index_at[main_axis] + 1) % result.shape[main_axis]] + index_at[main_axis + 1:]
    return result.at[tuple(index_at)].set(smallest).at[tuple(beside)].set(largest)


def block_levels(own_key, dims, cuts, low, largest):
    level, own = 1.0, jax.random.fold_in(own_key, 6)
    for dim, parts in cuts:
        draws = jnp.exp(jax.random.uniform(jax.random.fold_in(own, dim), (parts,), jnp.float32, low / len(cuts), largest / len(cuts)))
        level = level * jnp.repeat(draws, dims[dim] // parts).reshape([-1 if axis == dim else 1 for axis in range(len(dims))])
    return level


def assign_block(rng, own, number, rows, amount, top, reach, skew):
    sequence = jax.random.permutation(rng, amount)
    crowded, common = portions_of(amount, rows * top, reach, skew, True), portions_of(amount, rows * top, reach, skew, False)
    places = jnp.arange(amount)

    def named(sizes, rotation):
        used = int((sizes > 0).sum())
        fixed = max(1, used // 4)
        shifted = fixed + (places - fixed + rotation * (used - fixed)) % max(1, amount - fixed)
        return jnp.zeros((amount,), jnp.int32).at[sequence[jnp.where(places < fixed, places, shifted)]].set(jnp.asarray(sizes, jnp.int32))

    sizes = jnp.where(number % 4 == 0, named(crowded, number // 4), named(common, number - number // 4 - 1))
    mixed = jax.random.permutation(jax.random.fold_in(own, 3), amount)
    source_of, sink = mixed[0:amount // 2 * 2:2], mixed[1:amount // 2 * 2:2]
    slack = jnp.minimum(sizes[source_of] - 1, reach - sizes[sink]) // 2
    slack = jnp.where((source_of == sequence[0]) | (sink == sequence[0]) | (sizes[sink] == 0), 0, jnp.maximum(slack, 0))
    shifted = jax.random.randint(jax.random.fold_in(own, 4), (amount // 2,), 0, 1 << 20) % (slack + 1)
    sizes = sizes.at[source_of].add(-shifted).at[sink].add(shifted)
    items = jnp.searchsorted(jnp.cumsum(sizes), jnp.arange(rows * top), side="right").astype(jnp.int32)
    table = items.reshape(top, rows).T
    table = table[jax.random.permutation(jax.random.fold_in(own, 1), rows)]
    rotation = jax.random.randint(jax.random.fold_in(own, 2), (rows, 1), 0, top)
    return jnp.take_along_axis(table, (jnp.arange(top)[None, :] + rotation) % top, axis=1)


def portions_of(count, total, limit, skew, full):
    loads = [(1 << 20) // math.isqrt(rank ** skew) + 1 for rank in range(1, count + 1)]
    largest = limit if full else min(limit, max(-(-total // count), total * loads[0] // sum(loads)))
    least = 1 if total - largest >= count - 1 else 0
    holding, rest = [largest] + [least] * (count - 1), total - largest - least * (count - 1)
    while rest > 0:
        free = [i for i in range(1, count) if holding[i] < largest] or [i for i in range(1, count) if holding[i] < limit]
        whole, remaining = sum([loads[i] for i in free]), rest
        for i in free:
            addition = min(limit - holding[i], max(1, remaining * loads[i] // whole), rest)
            holding[i] = holding[i] + addition
            rest = rest - addition
    return np.array(holding)


def scatter_about(rng, dims, deviation, bound, cuts=(), held_as=jnp.bfloat16):
    entries = deviation * jax.random.normal(rng, dims, jnp.float32)
    if cuts:
        entries = entries * block_levels(rng, dims, cuts, -0.22, 0.18)
    return jnp.clip(entries, -bound, bound).astype(held_as)


def setup_inputs(seed: int = 0) -> dict:
    key_list = jax.random.split(jax.random.key(seed), 15)
    seal_state = scatter_about(key_list[0], (12, NC, NA), 1.0, 6.0, ((1, 8), (2, 4)), jnp.float32)
    seal_blocks = scatter_about(key_list[1], (5, 36, NC, NA), 0.15, 0.875, ((2, 8), (3, 4)))
    seal_scales = jnp.clip(jnp.exp(math.log(3.0) - 2.3025851 * jax.random.uniform(key_list[2], (5, NC, NA), jnp.float32) ** block_levels(key_list[2], (5, NC, NA), ((1, 8), (2, 4)), -0.2, 0.2)), 0.3, 3.0)
    seal_volume = jnp.clip(jnp.exp(math.log(3.0) - 2.3025851 * jax.random.uniform(key_list[3], (NC, NA), jnp.float32) ** block_levels(key_list[3], (NC, NA), ((0, 8), (1, 4)), -0.2, 0.2)), 0.3, 3.0)
    cavity_state = scatter_about(key_list[4], (12, NCAV), 1.0, 6.0, ((1, 32),), jnp.float32)
    cavity_blocks = scatter_about(key_list[5], (5, 36, NCAV), 0.15, 0.875, ((2, 32),))
    cavity_scales = jnp.clip(jnp.exp(math.log(3.0) - 2.3025851 * jax.random.uniform(key_list[6], (5, NCAV), jnp.float32) ** block_levels(key_list[6], (5, NCAV), ((1, 32),), -0.2, 0.2)), 0.3, 3.0)
    cavity_links = place_ends(jax.random.randint(key_list[7], (4, NCAV), 0, CV), jax.random.fold_in(key_list[7], 1), 0, CV - 1).astype(jnp.int32)
    cavity_volume = jnp.clip(jnp.exp(math.log(3.0) - 2.3025851 * jax.random.uniform(key_list[8], (NCAV,), jnp.float32) ** block_levels(key_list[8], (NCAV,), ((0, 32),), -0.2, 0.2)), 0.3, 3.0)
    link_owner_keys = jax.random.split(jax.random.fold_in(key_list[9], 1), NIF // IF_DEV)
    link_owner_turns = jax.random.permutation(jax.random.fold_in(key_list[9], 3), NIF // IF_DEV)
    link_owner = jax.vmap(lambda own, number: assign_block(jax.random.fold_in(key_list[9], 2), own, number, IF_DEV, N_CIRC, 1, CAP, 2))(link_owner_keys, link_owner_turns).reshape((NIF, 1))
    link_seal = place_ends(jax.random.randint(key_list[10], (NIF,), 0, CC * CA), jax.random.fold_in(key_list[10], 1), 0, (CC * CA) - 1).astype(jnp.int32)
    link_cavity = place_ends(jax.random.randint(key_list[11], (NIF,), 0, CV), jax.random.fold_in(key_list[11], 1), 0, CV - 1).astype(jnp.int32)
    link_blocks = scatter_about(key_list[12], (2, 36, NIF), 0.15, 0.875, ((2, 32),))
    link_scales = jnp.clip(jnp.exp(math.log(3.0) - 2.3025851 * jax.random.uniform(key_list[13], (2, NIF), jnp.float32) ** block_levels(key_list[13], (2, NIF), ((1, 32),), -0.2, 0.2)), 0.3, 3.0)
    return {"seal_state": seal_state, "seal_blocks": seal_blocks, "seal_scales": seal_scales, "seal_volume": seal_volume, "cavity_state": cavity_state, "cavity_blocks": cavity_blocks, "cavity_scales": cavity_scales, "cavity_links": cavity_links, "cavity_volume": cavity_volume, "link_owner": link_owner, "link_seal": link_seal, "link_cavity": link_cavity, "link_blocks": link_blocks, "link_scales": link_scales}


whirl_rate = 0.6


def block_product(blocks, factor, vector):
    real_rows = []
    imag_rows = []
    for out_row in range(6):
        leading = blocks[out_row * 6].astype(jnp.float32)
        real_part = leading * vector[0]
        imag_part = leading * vector[6]
        for in_col in range(1, 6):
            element = blocks[out_row * 6 + in_col].astype(jnp.float32)
            real_part = real_part + element * vector[in_col]
            imag_part = imag_part + element * vector[6 + in_col]
        real_rows.append(real_part)
        imag_rows.append(imag_part)
    return factor * jnp.stack(real_rows + imag_rows)


def whirl_term(vector, volume):
    weight = whirl_rate * volume
    return jnp.concatenate([-weight * vector[6:], weight * vector[:6]], axis=0)


def reference(seal_state, seal_blocks, seal_scales, seal_volume, cavity_state, cavity_blocks, cavity_scales, cavity_links, cavity_volume, link_owner, link_seal, link_cavity, link_blocks, link_scales):
    lower_axial = jnp.pad(seal_state, ((0, 0), (0, 0), (1, 0)))[:, :, :-1]
    upper_axial = jnp.pad(seal_state, ((0, 0), (0, 0), (0, 1)))[:, :, 1:]
    neighbours = (seal_state, jnp.roll(seal_state, 1, axis=1), jnp.roll(seal_state, -1, axis=1), lower_axial, upper_axial)
    seal_result = whirl_term(seal_state, seal_volume)
    for number in range(5):
        seal_result = seal_result + block_product(seal_blocks[number], seal_scales[number], neighbours[number])
    tiles = N_CIRC * N_AXIAL
    cavity_tiled = cavity_state.reshape(12, tiles, CV)
    links_tiled = cavity_links.reshape(4, tiles, CV)
    cavity_result = whirl_term(cavity_state, cavity_volume)
    cavity_result = cavity_result + block_product(cavity_blocks[0], cavity_scales[0], cavity_state)
    for number in range(4):
        gathered = jnp.take_along_axis(cavity_tiled, links_tiled[number][None], axis=2).reshape(12, -1)
        cavity_result = cavity_result + block_product(cavity_blocks[number + 1], cavity_scales[number + 1], gathered)
    row_ids = jnp.arange(NIF).astype(jnp.int32)
    tile_ids = row_ids // IF_DEV
    axial_ids = tile_ids % N_AXIAL
    seal_circ = link_owner[:, 0] * CC + link_seal // CA
    seal_axial = axial_ids * CA + link_seal % CA
    cavity_cells = tile_ids * CV + link_cavity
    cavity_values = cavity_state[:, cavity_cells]
    seal_values = seal_state[:, seal_circ, seal_axial]
    seal_result = seal_result.at[:, seal_circ, seal_axial].add(block_product(link_blocks[0], link_scales[0], cavity_values))
    cavity_result = cavity_result.at[:, cavity_cells].add(block_product(link_blocks[1], link_scales[1], seal_values))
    return seal_result, cavity_result
```

```python
import functools
import jax
import jax.numpy as jnp
from jax import lax
from jax.experimental import pallas as pl
from jax.experimental.pallas import tpu as pltpu
from jax.sharding import PartitionSpec as P

whirl_rate = 0.6
F32, BF16, I32 = jnp.float32, jnp.bfloat16, jnp.int32
LANES = 128
WIDE = 256
PARAMS = pltpu.CompilerParams(vmem_limit_bytes=40 * 1024 * 1024)
VMEM = pl.BlockSpec(memory_space=pltpu.VMEM)


def iota(shape, axis):
    return lax.broadcasted_iota(I32, shape, axis)


def lane_take(row, index):
    table = jnp.broadcast_to(row, index.shape)
    return jnp.take_along_axis(table, index, axis=1, mode="promise_in_bounds")


def halves(value):
    high = value.astype(BF16).astype(F32)
    return high, value - high


def product_into(totals, entry, factor, vector):
    for row in range(6):
        real_part = imag_part = None
        for col in range(6):
            element = entry(6 * row + col)
            real_term, imag_term = element * vector[col], element * vector[6 + col]
            real_part = real_term if real_part is None else real_part + real_term
            imag_part = imag_term if imag_part is None else imag_part + imag_term
        real_part, imag_part = factor * real_part, factor * imag_part
        totals[row] = real_part if totals[row] is None else totals[row] + real_part
        totals[6 + row] = imag_part if totals[6 + row] is None else totals[6 + row] + imag_part
    return totals


def whirl(vector, volume):
    weight = whirl_rate * volume
    return [-weight * v for v in vector[6:]] + [weight * v for v in vector[:6]]


def fold_cells(source, target, count, base, cells):
    rows = cells // LANES
    for chunk in range(rows):
        target[pl.ds(base + chunk, count, stride=rows), :] = source[:, chunk * LANES : (chunk + 1) * LANES]


def interface_kernel(
    sectors, halo_rows, owner, seal_index, cavity_index, state, blocks, scales, first, last,
    send, slots, block_rows, scale_rows, state_rows, left, right,
):
    rows = owner.shape[0]
    capacity = 2 * rows * LANES // sectors
    sector_id = iota((sectors, LANES), 0)
    hot = [
        jnp.where(sector_id == owner[c : c + 1, :], 1.0, 0.0).astype(F32) for c in range(rows)
    ]
    stacked = jnp.concatenate(hot, axis=0).astype(BF16)
    before = (iota((LANES, LANES), 0) < iota((LANES, LANES), 1)).astype(F32).astype(BF16)
    prefix = jnp.dot(stacked, before, preferred_element_type=F32)
    totals = jnp.dot(stacked, jnp.ones((LANES, LANES), BF16), preferred_element_type=F32)
    offset = jnp.zeros((sectors, LANES), F32)
    for c in range(rows):
        part = slice(c * sectors, (c + 1) * sectors)
        place = jnp.sum(hot[c] * (prefix[part] + offset), axis=0, keepdims=True)
        slots[c : c + 1, :] = owner[c : c + 1, :] * capacity + place.astype(I32)
        offset = offset + totals[part]
    for entry in range(36):
        both = blocks[entry].astype(F32)
        for c in range(rows):
            block_rows[pl.ds(entry * rows + c, 2, stride=36 * rows), :] = both[
                :, c * LANES : (c + 1) * LANES
            ]
    fold_cells(scales, scale_rows, 2, 0, rows * LANES)
    fold_cells(state, state_rows, 12, 0, state.shape[1])
    tile_rows = state.shape[1] // LANES
    cell = cavity_index[...]
    lane, high = cell & (LANES - 1), cell >> 7
    vector = [jnp.zeros((rows, LANES), F32)] * 12
    for r in range(tile_rows):
        here = high == r
        for f in range(12):
            row = state_rows[f * tile_rows + r : f * tile_rows + r + 1, :]
            vector[f] = jnp.where(here, lane_take(row, lane), vector[f])
    terms = product_into(
        [None] * 12, lambda e: block_rows[e * rows : (e + 1) * rows, :], scale_rows[0:rows, :], vector
    )
    terms.append(seal_index[...].astype(F32))
    parts = [half for term in terms for half in halves(term)]
    groups = 2 * rows * LANES // WIDE
    for c in range(rows):
        slot = slots[c : c + 1, :]
        cols = slice(c * LANES, (c + 1) * LANES)
        right[:, cols] = jnp.where(
            iota((WIDE, LANES), 0) == (slot & (WIDE - 1)), 1.0, 0.0
        ).astype(BF16)
        here = iota((groups, LANES), 0) == (slot >> 8)
        for number, part in enumerate(parts):
            left[number * groups : (number + 1) * groups, cols] = jnp.where(
                here, part[c : c + 1, :], 0.0
            ).astype(BF16)
    moved = lax.dot_general(
        left[...], right[...], (((1,), (1,)), ((), ())), preferred_element_type=F32
    )
    for number in range(13):
        pair = moved[2 * number * groups : (2 * number + 2) * groups]
        value = pair[:groups] + pair[groups:]
        for half in range(2):
            send[pl.ds(half * 16 + number, groups, stride=32), :] = value[
                :, half * LANES : (half + 1) * LANES
            ]
    for number in range(13, 16):
        send[pl.ds(number, 2 * groups, stride=16), :] = jnp.zeros((2 * groups, LANES), F32)
    if halo_rows:
        me = lax.axis_index("circ")
        for step, edge, row in ((1, last, 7), (sectors - 1, first, 0)):
            base = lax.rem(me + step, sectors) * 64
            for f in range(12):
                send[pl.ds(base + (f // 3) * 16 + 13 + f % 3, 1), :] = edge[f, row : row + 1, :]


def face_kernel(state, faces):
    lane = iota(faces.shape, 1)
    total = jnp.zeros(faces.shape, F32)
    for f in range(12):
        total = jnp.where(lane == f, pltpu.roll(state[f], f + 1, 1), total)
        total = jnp.where(lane == 16 + f, pltpu.roll(state[f], 16 + f, 1), total)
    faces[...] = total


def seal_kernel(step_rows, state, blocks, scales, volume, from_low, from_high, out, beside, along):
    rows = state.shape[1]

    @pl.when(pl.program_id(0) == 0)
    def _():
        lane = iota((rows, LANES), 1)
        low, high = from_low[...], from_high[...]
        for f in range(12):
            beside[0, f, 1:rows, :] = state[f, 0 : rows - 1, :]
            beside[0, f, 0:1, :] = jnp.zeros((1, LANES), F32)
            beside[1, f, 0 : rows - 1, :] = state[f, 1:rows, :]
            beside[1, f, rows - 1 : rows, :] = jnp.zeros((1, LANES), F32)
            own = state[f]
            edge = pltpu.roll(low, (LANES - f) % LANES, 1)
            along[0, f] = jnp.where(lane == 0, edge, pltpu.roll(own, 1, 1))
            edge = pltpu.roll(high, LANES - 1 - 16 - f, 1)
            along[1, f] = jnp.where(lane == LANES - 1, edge, pltpu.roll(own, LANES - 1, 1))

    start = pl.multiple_of(pl.program_id(0) * step_rows, step_rows)
    here = pl.ds(start, step_rows)
    own = [state[f, here, :] for f in range(12)]
    totals = whirl(own, volume[here, :])
    for number in range(5):
        if number == 0:
            vector = own
        else:
            source = beside if number < 3 else along
            vector = [source[(number - 1) % 2, f, here, :] for f in range(12)]
        totals = product_into(
            totals, lambda e: blocks[number, e].astype(F32), scales[number, here, :], vector
        )
    for f in range(12):
        out[f] = totals[f]


def answer_kernel(state, arrived, send):
    chunks = arrived.shape[0] // 16
    cell = arrived[pl.ds(12, chunks, stride=16), :].astype(I32)
    lane, high = cell & (LANES - 1), cell >> 7
    value = [jnp.zeros(cell.shape, F32)] * 12
    for r in range(state.shape[1]):
        here = high == r
        for f in range(12):
            value[f] = jnp.where(here, lane_take(state[f, r : r + 1, :], lane), value[f])
    for f in range(12):
        send[pl.ds(f, chunks, stride=12), :] = value[f]


def seal_add_kernel(
    halo_rows, sectors, part, arrived, blocks_low, blocks_high, scales, halo_low, halo_high,
    out, left, right, total,
):
    chunks = arrived.shape[0] // 16
    rows = part.shape[1]
    half_rows = rows // 2
    total[...] = jnp.zeros_like(total)
    deep = left.shape[1] // LANES

    def add_chunks(step, carry):
        for sub in range(deep):
            tile = arrived[pl.ds(pl.multiple_of((step * deep + sub) * 16, 16), 16), :]
            high, low = halves(tile)
            cell = tile[12:13, :].astype(I32)
            row = cell >> 7
            column = (cell & (LANES - 1)) + jnp.where(row >= half_rows, LANES, 0)
            row = jnp.where(row >= half_rows, row - half_rows, row)
            cols = slice(sub * LANES, (sub + 1) * LANES)
            right[:, cols] = jnp.where(iota((WIDE, LANES), 0) == column, 1.0, 0.0).astype(BF16)
            here = iota((half_rows, LANES), 0) == row
            for f in range(12):
                for number, source in enumerate((high, low)):
                    at = (2 * f + number) * half_rows
                    left[at : at + half_rows, cols] = jnp.where(
                        here, source[f : f + 1, :], 0.0
                    ).astype(BF16)
        total[...] += lax.dot_general(
            left[...], right[...], (((1,), (1,)), ((), ())), preferred_element_type=F32
        )
        return carry

    lax.fori_loop(0, chunks // deep, add_chunks, 0)
    for f in range(12):
        added = (
            total[2 * f * half_rows : (2 * f + 1) * half_rows, :]
            + total[(2 * f + 1) * half_rows : (2 * f + 2) * half_rows, :]
        )
        out[f, 0:half_rows, :] = part[f, 0:half_rows, :] + added[:, :LANES]
        out[f, half_rows:rows, :] = part[f, half_rows:rows, :] + added[:, LANES:]
    me = lax.axis_index("circ")
    edge = blocks_low.shape[2]
    for number, step, halo, blocks in ((1, sectors - 1, halo_low, blocks_low), (2, 1, halo_high, blocks_high)):
        if halo_rows:
            base = lax.rem(me + step, sectors) * 64
            vector = [
                arrived[pl.ds(base + (f // 3) * 16 + 13 + f % 3, 1), :] for f in range(12)
            ]
        else:
            vector = [halo[f] for f in range(12)]
        at = 0 if number == 1 else rows - 1
        inner = 0 if number == 1 else edge - 1
        terms = product_into(
            [None] * 12,
            lambda e: blocks[0, e].astype(F32)[inner : inner + 1, :],
            scales[number, at : at + 1, :],
            vector,
        )
        for f in range(12):
            out[f, at : at + 1, :] = out[f, at : at + 1, :] + terms[f]


def cavity_kernel(
    state, blocks, scales, links, volume, link_blocks,
    out, link_rows, state_rows, block_rows, scale_rows, face_rows, out_rows,
):
    cells = state.shape[1]
    rows = cells // LANES
    fold_cells(state, state_rows, 12, 0, cells)
    fold_cells(scales, scale_rows, 5, 0, cells)
    fold_cells(links, face_rows, 4, 0, cells)
    for number in range(5):
        for c in range(rows):
            block_rows[pl.ds(number * 36 * rows + c, 36, stride=rows), :] = blocks[
                number, :, c * LANES : (c + 1) * LANES
            ].astype(F32)
    own = [state_rows[f * rows : (f + 1) * rows, :] for f in range(12)]
    totals = whirl(own, volume[...])
    for number in range(5):
        if number == 0:
            vector = own
        else:
            cell = face_rows[(number - 1) * rows : number * rows, :]
            lane, high = cell & (LANES - 1), cell >> 7
            vector = [jnp.zeros((rows, LANES), F32)] * 12
            for r in range(rows):
                here = high == r
                for f in range(12):
                    row = state_rows[f * rows + r : f * rows + r + 1, :]
                    vector[f] = jnp.where(here, lane_take(row, lane), vector[f])
        base = number * 36 * rows
        totals = product_into(
            totals,
            lambda e: block_rows[base + e * rows : base + (e + 1) * rows, :],
            scale_rows[number * rows : (number + 1) * rows, :],
            vector,
        )
    for f in range(12):
        out_rows[f * rows : (f + 1) * rows, :] = totals[f]
    for c in range(rows):
        out[:, c * LANES : (c + 1) * LANES] = out_rows[pl.ds(c, 12, stride=rows), :]
    row_count = link_blocks.shape[2] // LANES
    for entry in range(36):
        both = link_blocks[entry].astype(F32)
        for c in range(row_count):
            link_rows[entry * row_count + c : entry * row_count + c + 1, :] = both[
                1:2, c * LANES : (c + 1) * LANES
            ]


def cavity_add_kernel(
    part, arrived, slots, cavity_index, link_rows, scales, out, scale_rows, left, right
):
    rows = slots.shape[0]
    chunks = arrived.shape[0] // 12
    slot = slots[...]
    lane, high = slot & (LANES - 1), slot >> 7
    vector = [jnp.zeros(slot.shape, F32)] * 12
    for chunk in range(chunks):
        here = high == chunk
        for f in range(12):
            row = arrived[chunk * 12 + f : chunk * 12 + f + 1, :]
            vector[f] = jnp.where(here, lane_take(row, lane), vector[f])
    fold_cells(scales, scale_rows, 2, 0, rows * LANES)
    terms = product_into(
        [None] * 12,
        lambda e: link_rows[e * rows : (e + 1) * rows, :],
        scale_rows[rows : 2 * rows, :],
        vector,
    )
    parts = [halves(term) for term in terms]
    bands = part.shape[1] // WIDE
    for c in range(rows):
        cell = cavity_index[c : c + 1, :]
        cols = slice(c * LANES, (c + 1) * LANES)
        right[:, cols] = jnp.where(iota((WIDE, LANES), 0) == (cell & (WIDE - 1)), 1.0, 0.0).astype(BF16)
        band = cell >> 8
        zero = jnp.zeros((4, LANES), F32)
        tile = jnp.concatenate(
            [p[0][c : c + 1, :] for p in parts] + [zero] + [p[1][c : c + 1, :] for p in parts] + [zero],
            axis=0,
        )
        for b in range(bands):
            left[b * 32 : (b + 1) * 32, cols] = jnp.where(band == b, tile, 0.0).astype(BF16)
    added = lax.dot_general(
        left[...], right[...], (((1,), (1,)), ((), ())), preferred_element_type=F32
    )
    for b in range(bands):
        cols = slice(b * WIDE, (b + 1) * WIDE)
        out[:, cols] = part[:, cols] + (added[b * 32 : b * 32 + 12] + added[b * 32 + 16 : b * 32 + 28])


def exchange(values, sectors, features):
    chunks = values.shape[0] // features
    if sectors <= chunks:
        shaped = values.reshape(sectors, chunks // sectors * features, LANES)
        moved = lax.all_to_all(shaped, "circ", split_axis=0, concat_axis=0, tiled=True)
        return moved.reshape(values.shape)
    each = sectors // chunks
    shaped = values.reshape(chunks, features, each, LANES // each).transpose(0, 2, 1, 3)
    shaped = shaped.reshape(sectors, features, LANES // each)
    moved = lax.all_to_all(shaped, "circ", split_axis=0, concat_axis=0, tiled=True)
    moved = moved.reshape(chunks, each, features, LANES // each).transpose(0, 2, 1, 3)
    return moved.reshape(values.shape)


def on_device(
    seal_state,
    seal_blocks,
    seal_scales,
    seal_volume,
    cavity_state,
    cavity_blocks,
    cavity_scales,
    cavity_links,
    cavity_volume,
    link_owner,
    link_seal,
    link_cavity,
    link_blocks,
    link_scales,
):
    sectors = lax.axis_size("circ")
    segments = lax.axis_size("axial")
    _, seal_rows, _ = seal_state.shape
    cells = cavity_state.shape[1]
    count = link_seal.shape[0]
    rows = count // LANES
    groups = 2 * count // WIDE
    halo_rows = sectors * 2 == groups
    shape = jax.ShapeDtypeStruct
    owner = link_owner.reshape(rows, LANES)
    seal_index = link_seal.reshape(rows, LANES)
    cavity_index = link_cavity.reshape(rows, LANES)
    pair_blocks = link_blocks.transpose(1, 0, 2)

    edge = lambda at: pl.BlockSpec((12, 8, LANES), lambda i: (0, at, 0))
    whole = lambda a: pl.BlockSpec(a.shape, lambda i: (0,) * len(a.shape))
    head = (owner, seal_index, cavity_index, cavity_state, pair_blocks, link_scales)
    send, slots = pl.pallas_call(
        functools.partial(interface_kernel, sectors, halo_rows),
        grid=(1,),
        in_specs=[whole(a) for a in head] + [edge(0), edge(seal_rows // 8 - 1)],
        out_specs=[
            pl.BlockSpec((groups * 32, LANES), lambda i: (0, 0)),
            pl.BlockSpec((rows, LANES), lambda i: (0, 0)),
        ],
        out_shape=[shape((groups * 32, LANES), F32), shape((rows, LANES), I32)],
        scratch_shapes=[
            pltpu.VMEM((72 * rows, LANES), F32),
            pltpu.VMEM((2 * rows, LANES), F32),
            pltpu.VMEM((12 * cells // LANES, LANES), F32),
            pltpu.VMEM((26 * groups, count), BF16),
            pltpu.VMEM((WIDE, count), BF16),
        ],
        compiler_params=PARAMS,
        name="interface",
    )(*head, seal_state, seal_state)
    arrived = exchange(send, sectors, 16)

    faces = pl.pallas_call(
        face_kernel,
        in_specs=[VMEM],
        out_specs=VMEM,
        out_shape=shape((seal_rows, LANES), F32),
        compiler_params=PARAMS,
        name="faces",
    )(seal_state)
    from_low = lax.ppermute(faces, "axial", [(i, i + 1) for i in range(segments - 1)])
    from_high = lax.ppermute(faces, "axial", [(i + 1, i) for i in range(segments - 1)])
    if halo_rows:
        halos = ()
    else:
        first, last = seal_state[:, :1], seal_state[:, -1:]
        halos = (
            lax.ppermute(last, "circ", [(i, (i + 1) % sectors) for i in range(sectors)]),
            lax.ppermute(first, "circ", [((i + 1) % sectors, i) for i in range(sectors)]),
        )

    cavity_part, link_rows = pl.pallas_call(
        cavity_kernel,
        in_specs=[VMEM] * 6,
        out_specs=[VMEM, VMEM],
        out_shape=[shape((12, cells), F32), shape((36 * rows, LANES), F32)],
        scratch_shapes=[
            pltpu.VMEM((12 * cells // LANES, LANES), F32),
            pltpu.VMEM((180 * cells // LANES, LANES), F32),
            pltpu.VMEM((5 * cells // LANES, LANES), F32),
            pltpu.VMEM((4 * cells // LANES, LANES), I32),
            pltpu.VMEM((12 * cells // LANES, LANES), F32),
        ],
        compiler_params=PARAMS,
        cost_estimate=pl.CostEstimate(flops=10**6, bytes_accessed=10**7, transcendentals=0),
        name="cavity",
    )(cavity_state, cavity_blocks, cavity_scales, cavity_links, cavity_volume.reshape(-1, LANES), pair_blocks)

    step_rows = 16
    seal_part = pl.pallas_call(
        functools.partial(seal_kernel, step_rows),
        grid=(seal_rows // step_rows,),
        in_specs=[
            whole(seal_state),
            pl.BlockSpec((5, 36, step_rows, LANES), lambda i: (0, 0, i, 0)),
            whole(seal_scales),
            whole(seal_volume),
            whole(faces),
            whole(faces),
        ],
        out_specs=pl.BlockSpec((12, step_rows, LANES), lambda i: (0, i, 0)),
        out_shape=shape(seal_state.shape, F32),
        scratch_shapes=[
            pltpu.VMEM((2,) + seal_state.shape, F32),
            pltpu.VMEM((2,) + seal_state.shape, F32),
        ],
        compiler_params=PARAMS,
        cost_estimate=pl.CostEstimate(flops=10**6, bytes_accessed=10**7, transcendentals=0),
        name="seal",
    )(seal_state, seal_blocks, seal_scales, seal_volume, from_low, from_high)

    answers = pl.pallas_call(
        answer_kernel,
        in_specs=[VMEM] * 2,
        out_specs=VMEM,
        out_shape=shape((groups * 24, LANES), F32),
        compiler_params=PARAMS,
        name="answers",
    )(seal_state, arrived)
    returned = exchange(answers, sectors, 12)

    near = lambda number, at: pl.BlockSpec((1, 36, 16, LANES), lambda i: (number, 0, at, 0))
    deep = 4
    halo_operands = halos if halos else (seal_scales[0, :1], seal_scales[0, :1])
    seal_result = pl.pallas_call(
        functools.partial(seal_add_kernel, halo_rows, sectors),
        grid=(1,),
        in_specs=[whole(seal_part), whole(arrived), near(1, 0), near(2, seal_rows // 16 - 1), whole(seal_scales)]
        + [whole(h) for h in halo_operands],
        out_specs=pl.BlockSpec(seal_part.shape, lambda i: (0, 0, 0)),
        out_shape=shape(seal_state.shape, F32),
        scratch_shapes=[
            pltpu.VMEM((12 * seal_rows, deep * LANES), BF16),
            pltpu.VMEM((WIDE, deep * LANES), BF16),
            pltpu.VMEM((12 * seal_rows, WIDE), F32),
        ],
        compiler_params=PARAMS,
        cost_estimate=pl.CostEstimate(flops=10**6, bytes_accessed=10**7, transcendentals=0),
        name="seal_add",
    )(seal_part, arrived, seal_blocks, seal_blocks, seal_scales, *halo_operands)

    cavity_result = pl.pallas_call(
        cavity_add_kernel,
        in_specs=[VMEM] * 6,
        out_specs=VMEM,
        out_shape=shape((12, cells), F32),
        scratch_shapes=[
            pltpu.VMEM((2 * rows, LANES), F32),
            pltpu.VMEM((32 * cells // WIDE, count), BF16),
            pltpu.VMEM((WIDE, count), BF16),
        ],
        compiler_params=PARAMS,
        name="cavity_add",
    )(cavity_part, returned, slots, cavity_index, link_rows, link_scales)
    return seal_result, cavity_result


def solution(mesh):
    return jax.shard_map(
        on_device,
        mesh=mesh,
        in_specs=(
            P(None, "circ", "axial"),
            P(None, None, "circ", "axial"),
            P(None, "circ", "axial"),
            P("circ", "axial"),
            P(None, ("circ", "axial")),
            P(None, None, ("circ", "axial")),
            P(None, ("circ", "axial")),
            P(None, ("circ", "axial")),
            P(("circ", "axial")),
            P(("circ", "axial"), None),
            P(("circ", "axial")),
            P(("circ", "axial")),
            P(None, None, ("circ", "axial")),
            P(None, ("circ", "axial")),
        ),
        out_specs=(P(None, "circ", "axial"), P(None, ("circ", "axial"))),
        check_vma=False,
    )
```

```python
import functools
import jax
import jax.numpy as jnp
from jax import lax
from jax.experimental import pallas as pl
from jax.experimental.pallas import tpu as pltpu
from jax.sharding import PartitionSpec as P

whirl_rate = 0.6
F32, BF16, I32 = jnp.float32, jnp.bfloat16, jnp.int32
LANES = 128
WIDE = 256
PARAMS = pltpu.CompilerParams(vmem_limit_bytes=16 * 1024 * 1024)
VMEM = pl.BlockSpec(memory_space=pltpu.VMEM)
HBM = pl.BlockSpec(memory_space=pltpu.HBM)


def iota(shape, axis):
    return lax.broadcasted_iota(I32, shape, axis)


def lane_take(row, index):
    table = jnp.broadcast_to(row, index.shape)
    return jnp.take_along_axis(table, index, axis=1, mode="promise_in_bounds")


def one_hot(index):
    return jnp.where(iota((WIDE, index.shape[1]), 0) == index, 1.0, 0.0).astype(BF16)


def halves(value):
    high = value.astype(BF16).astype(F32)
    return high, value - high


def product_into(totals, entry, factor, vector):
    for row in range(6):
        real_part = imag_part = None
        for col in range(6):
            element = entry(6 * row + col)
            real_term, imag_term = element * vector[col], element * vector[6 + col]
            real_part = real_term if real_part is None else real_part + real_term
            imag_part = imag_term if imag_part is None else imag_part + imag_term
        real_part, imag_part = factor * real_part, factor * imag_part
        totals[row] = real_part if totals[row] is None else totals[row] + real_part
        totals[6 + row] = imag_part if totals[6 + row] is None else totals[6 + row] + imag_part
    return totals


def whirl(vector, volume):
    weight = whirl_rate * volume
    return [-weight * v for v in vector[6:]] + [weight * v for v in vector[:6]]


def fold_cells(source, target, count, base, cells):
    rows = cells // LANES
    for chunk in range(rows):
        target[pl.ds(base + chunk, count, stride=rows), :] = source[:, chunk * LANES : (chunk + 1) * LANES]


def interface_kernel(
    sectors, halo_rows, owner_hbm, seal_index_hbm, cavity_index_hbm, state_hbm, blocks_hbm,
    scales_hbm, seal_hbm, send, slots, block_rows, scale_rows, state_rows, left, right,
    owner, seal_index, cavity_index, state, blocks, scales, first, last, arrivals,
):
    last_row = seal_hbm.shape[1]
    loads = start_loads(
        (
            (owner_hbm, owner),
            (blocks_hbm, blocks),
            (scales_hbm, scales),
            (state_hbm, state),
            (cavity_index_hbm, cavity_index),
            (seal_index_hbm, seal_index),
            (seal_hbm.at[:, 0:8, :], first),
            (seal_hbm.at[:, last_row - 8 : last_row, :], last),
        ),
        arrivals,
    )
    loads[0].wait()
    rows = owner.shape[0]
    capacity = 2 * rows * LANES // sectors
    sector_id = iota((sectors, LANES), 0)
    hot = [
        jnp.where(sector_id == owner[c : c + 1, :], 1.0, 0.0).astype(F32) for c in range(rows)
    ]
    stacked = jnp.concatenate(hot, axis=0).astype(BF16)
    before = (iota((LANES, LANES), 0) < iota((LANES, LANES), 1)).astype(F32).astype(BF16)
    prefix = jnp.dot(stacked, before, preferred_element_type=F32)
    totals = jnp.dot(stacked, jnp.ones((LANES, LANES), BF16), preferred_element_type=F32)
    offset = jnp.zeros((sectors, LANES), F32)
    for c in range(rows):
        part = slice(c * sectors, (c + 1) * sectors)
        place = jnp.sum(hot[c] * (prefix[part] + offset), axis=0, keepdims=True)
        slots[c : c + 1, :] = owner[c : c + 1, :] * capacity + place.astype(I32)
        offset = offset + totals[part]
    for load in loads[1:]:
        load.wait()
    for entry in range(36):
        both = blocks[entry].astype(F32)
        for c in range(rows):
            block_rows[pl.ds(entry * rows + c, 2, stride=36 * rows), :] = both[
                :, c * LANES : (c + 1) * LANES
            ]
    fold_cells(scales, scale_rows, 2, 0, rows * LANES)
    fold_cells(state, state_rows, 12, 0, state.shape[1])
    tile_rows = state.shape[1] // LANES
    cell = cavity_index[...]
    lane, high = cell & (LANES - 1), cell >> 7
    vector = [jnp.zeros((rows, LANES), F32)] * 12
    for r in range(tile_rows):
        here = high == r
        for f in range(12):
            row = state_rows[f * tile_rows + r : f * tile_rows + r + 1, :]
            vector[f] = jnp.where(here, lane_take(row, lane), vector[f])
    terms = product_into(
        [None] * 12, lambda e: block_rows[e * rows : (e + 1) * rows, :], scale_rows[0:rows, :], vector
    )
    terms.append(seal_index[...].astype(F32))
    parts = [half for term in terms for half in halves(term)]
    groups = 2 * rows * LANES // WIDE
    for c in range(rows):
        slot = slots[c : c + 1, :]
        cols = slice(c * LANES, (c + 1) * LANES)
        right[:, cols] = one_hot(slot & (WIDE - 1))
        here = iota((groups, LANES), 0) == (slot >> 8)
        for number, part in enumerate(parts):
            left[number * groups : (number + 1) * groups, cols] = jnp.where(
                here, part[c : c + 1, :], 0.0
            ).astype(BF16)
    moved = lax.dot_general(
        left[...], right[...], (((1,), (1,)), ((), ())), preferred_element_type=F32
    )
    for number in range(13):
        pair = moved[2 * number * groups : (2 * number + 2) * groups]
        value = pair[:groups] + pair[groups:]
        for half in range(2):
            send[pl.ds(half * 16 + number, groups, stride=32), :] = value[
                :, half * LANES : (half + 1) * LANES
            ]
    for number in range(13, 16):
        send[pl.ds(number, 2 * groups, stride=16), :] = jnp.zeros((2 * groups, LANES), F32)
    if halo_rows:
        me = lax.axis_index("circ")
        for step, edge, row in ((1, last, 7), (sectors - 1, first, 0)):
            base = lax.rem(me + step, sectors) * 64
            for f in range(12):
                send[pl.ds(base + (f // 3) * 16 + 13 + f % 3, 1), :] = edge[f, row : row + 1, :]


def start_loads(pairs, arrivals):
    loads = [
        pltpu.make_async_copy(source, target, arrivals.at[number])
        for number, (source, target) in enumerate(pairs)
    ]
    for load in loads:
        load.start()
    return loads


def face_kernel(state_hbm, faces, state, table, arrivals):
    (load,) = start_loads([(state_hbm, state)], arrivals)
    load.wait()
    lane = iota(faces.shape, 1)
    half_rows = faces.shape[0] // 2
    total = jnp.zeros(faces.shape, F32)
    for f in range(12):
        own = state[f]
        total = jnp.where(lane == f, pltpu.roll(own, f + 1, 1), total)
        total = jnp.where(lane == 16 + f, pltpu.roll(own, 16 + f, 1), total)
        at = pl.ds(f * half_rows, half_rows)
        for half in range(2):
            high, low = halves(own[half * half_rows : (half + 1) * half_rows, :])
            table[0, at, half * LANES : (half + 1) * LANES] = high.astype(BF16)
            table[1, at, half * LANES : (half + 1) * LANES] = low.astype(BF16)
    faces[...] = total


def seal_kernel(step_rows, state, blocks, scales, volume, inner, outer, out, edges, beside, along):
    rows = state.shape[1]
    lane = iota((rows, LANES), 1)
    odd = lax.rem(lax.axis_index("axial"), 2) == 1
    low = jnp.where(odd, inner[...], outer[...])
    high = jnp.where(odd, outer[...], inner[...])
    for f in range(12):
        beside[0, f, 1:rows, :] = state[f, 0 : rows - 1, :]
        beside[0, f, 0:1, :] = jnp.zeros((1, LANES), F32)
        beside[1, f, 0 : rows - 1, :] = state[f, 1:rows, :]
        beside[1, f, rows - 1 : rows, :] = jnp.zeros((1, LANES), F32)
        own = state[f]
        edge = pltpu.roll(low, (LANES - f) % LANES, 1)
        along[0, f] = jnp.where(lane == 0, edge, pltpu.roll(own, 1, 1))
        edge = pltpu.roll(high, LANES - 1 - 16 - f, 1)
        along[1, f] = jnp.where(lane == LANES - 1, edge, pltpu.roll(own, LANES - 1, 1))

    def add_rows(step, carry):
        here = pl.ds(pl.multiple_of(step * step_rows, step_rows), step_rows)
        own = [state[f, here, :] for f in range(12)]
        totals = whirl(own, volume[here, :])
        for number in range(5):
            if number == 0:
                vector = own
            else:
                source = beside if number < 3 else along
                vector = [source[(number - 1) % 2, f, here, :] for f in range(12)]
            totals = product_into(
                totals, lambda e: blocks[number, e, here, :].astype(F32), scales[number, here, :], vector
            )
        for f in range(12):
            out[f, here, :] = totals[f]
        return carry

    lax.fori_loop(0, rows // step_rows, add_rows, 0)
    for number, near, at in ((1, 0, 0), (2, rows - 16, 15)):
        first = (number - 1) * 40
        for e in range(36):
            tile = blocks[number, e, near : near + 16, :].astype(F32)
            edges[first + e : first + e + 1, :] = tile[at : at + 1, :]
        edges[first + 36 : first + 37, :] = scales[number, near + at : near + at + 1, :]
        edges[first + 37 : first + 40, :] = jnp.zeros((3, LANES), F32)


def pick(table, hot, here):
    found = jnp.dot(table[0], hot, preferred_element_type=F32)
    found = found + jnp.dot(table[1], hot, preferred_element_type=F32)
    bands = here.shape[0]
    return [
        jnp.sum(jnp.where(here, found[f * bands : (f + 1) * bands, :], 0.0), axis=0, keepdims=True)
        for f in range(12)
    ]


def answer_kernel(width, table, arrived, send_hbm, send, sent):
    chunks = arrived.shape[0] // 16
    half_rows = table.shape[1] // 12
    copies = []
    for base in range(0, chunks, width):
        cell = jnp.concatenate(
            [arrived[g * 16 + 12 : g * 16 + 13, :] for g in range(base, base + width)], axis=1
        ).astype(I32)
        row = cell >> 7
        upper = row >= half_rows
        index = (cell & (LANES - 1)) + jnp.where(upper, LANES, 0)
        row = row - jnp.where(upper, half_rows, 0)
        here = iota((half_rows, width * LANES), 0) == row
        value = pick(table, one_hot(index), here)
        for f in range(12):
            for part in range(width):
                at = (base + part) * 12 + f
                send[at : at + 1, :] = value[f][:, part * LANES : (part + 1) * LANES]
        done = pl.ds(base * 12, width * 12)
        copies.append(
            pltpu.make_async_copy(send.at[done, :], send_hbm.at[done, :], sent.at[base // width])
        )
        copies[-1].start()
    for copy in copies:
        copy.wait()


def seal_add_kernel(
    halo_rows, sectors, part, arrived, edges, slots, cavity_index,
    *refs,
):
    *halos, out, slot_hot, cell_hot, left, right, total = refs
    chunks = arrived.shape[0] // 16
    rows = part.shape[1]
    half_rows = rows // 2
    total[...] = jnp.zeros_like(total)
    deep = left.shape[1] // LANES

    def add_chunks(step, carry):
        for sub in range(deep):
            tile = arrived[pl.ds(pl.multiple_of((step * deep + sub) * 16, 16), 16), :]
            high, low = halves(tile)
            cell = tile[12:13, :].astype(I32)
            row = cell >> 7
            column = (cell & (LANES - 1)) + jnp.where(row >= half_rows, LANES, 0)
            row = jnp.where(row >= half_rows, row - half_rows, row)
            cols = slice(sub * LANES, (sub + 1) * LANES)
            right[:, cols] = one_hot(column)
            here = iota((half_rows, LANES), 0) == row
            for f in range(12):
                for number, source in enumerate((high, low)):
                    at = (2 * f + number) * half_rows
                    left[at : at + half_rows, cols] = jnp.where(
                        here, source[f : f + 1, :], 0.0
                    ).astype(BF16)
        total[...] += lax.dot_general(
            left[...], right[...], (((1,), (1,)), ((), ())), preferred_element_type=F32
        )
        return carry

    for c in range(slots.shape[0]):
        cols = slice(c * LANES, (c + 1) * LANES)
        for source, target in ((slots, slot_hot), (cavity_index, cell_hot)):
            target[:, cols] = one_hot(source[c : c + 1, :] & (WIDE - 1))
    lax.fori_loop(0, chunks // deep, add_chunks, 0)
    for f in range(12):
        added = (
            total[2 * f * half_rows : (2 * f + 1) * half_rows, :]
            + total[(2 * f + 1) * half_rows : (2 * f + 2) * half_rows, :]
        )
        out[f, 0:half_rows, :] = part[f, 0:half_rows, :] + added[:, :LANES]
        out[f, half_rows:rows, :] = part[f, half_rows:rows, :] + added[:, LANES:]
    me = lax.axis_index("circ")
    for number, step in ((1, sectors - 1), (2, 1)):
        if halo_rows:
            base = lax.rem(me + step, sectors) * 64
            vector = [
                arrived[pl.ds(base + (f // 3) * 16 + 13 + f % 3, 1), :] for f in range(12)
            ]
        else:
            vector = [halos[number - 1][f] for f in range(12)]
        at = 0 if number == 1 else rows - 1
        first = (number - 1) * 40
        terms = product_into(
            [None] * 12,
            lambda e: edges[first + e : first + e + 1, :],
            edges[first + 36 : first + 37, :],
            vector,
        )
        for f in range(12):
            out[f, at : at + 1, :] = out[f, at : at + 1, :] + terms[f]


def cavity_kernel(
    state_hbm, blocks_hbm, scales_hbm, links_hbm, volume_hbm, link_blocks_hbm, link_scales_hbm,
    index_hbm, seal_blocks_hbm, seal_scales_hbm, seal_volume_hbm,
    out, link_rows, link_scale_rows, cavity_index, seal_blocks, seal_scales, seal_volume,
    state_rows, block_rows, scale_rows, face_rows, out_rows,
    state, blocks, scales, links, volume, link_blocks, link_scales, arrivals,
):
    loads = start_loads(
        (
            (state_hbm, state),
            (links_hbm, links),
            (blocks_hbm, blocks),
            (scales_hbm, scales),
            (volume_hbm, volume),
            (link_blocks_hbm, link_blocks),
            (link_scales_hbm, link_scales),
            (index_hbm, cavity_index),
            (seal_scales_hbm, seal_scales),
            (seal_volume_hbm, seal_volume),
            (seal_blocks_hbm, seal_blocks),
        ),
        arrivals,
    )
    for load in loads[:7]:
        load.wait()
    cells = state.shape[1]
    rows = cells // LANES
    fold_cells(state, state_rows, 12, 0, cells)
    fold_cells(scales, scale_rows, 5, 0, cells)
    fold_cells(links, face_rows, 4, 0, cells)
    for number in range(5):
        for c in range(rows):
            block_rows[pl.ds(number * 36 * rows + c, 36, stride=rows), :] = blocks[
                number, :, c * LANES : (c + 1) * LANES
            ].astype(F32)
    own = [state_rows[f * rows : (f + 1) * rows, :] for f in range(12)]
    totals = whirl(own, volume[...])
    for number in range(5):
        if number == 0:
            vector = own
        else:
            cell = face_rows[(number - 1) * rows : number * rows, :]
            lane, high = cell & (LANES - 1), cell >> 7
            vector = [jnp.zeros((rows, LANES), F32)] * 12
            for r in range(rows):
                here = high == r
                for f in range(12):
                    row = state_rows[f * rows + r : f * rows + r + 1, :]
                    vector[f] = jnp.where(here, lane_take(row, lane), vector[f])
        base = number * 36 * rows
        totals = product_into(
            totals,
            lambda e: block_rows[base + e * rows : base + (e + 1) * rows, :],
            scale_rows[number * rows : (number + 1) * rows, :],
            vector,
        )
    for f in range(12):
        out_rows[f * rows : (f + 1) * rows, :] = totals[f]
    for c in range(rows):
        out[:, c * LANES : (c + 1) * LANES] = out_rows[pl.ds(c, 12, stride=rows), :]
    row_count = link_blocks.shape[2] // LANES
    for entry in range(36):
        both = link_blocks[entry].astype(F32)
        for c in range(row_count):
            link_rows[entry * row_count + c : entry * row_count + c + 1, :] = both[
                1:2, c * LANES : (c + 1) * LANES
            ]
    fold_cells(link_scales, link_scale_rows, 2, 0, row_count * LANES)
    for load in loads[7:]:
        load.wait()


def cavity_add_kernel(
    width, part, arrived, slots, cavity_index, link_rows, scale_rows, slot_hot, cell_hot,
    out, left, table, found,
):
    rows = slots.shape[0]
    chunks = arrived.shape[0] // 12
    groups = chunks // 2
    for f in range(12):
        for half in range(2):
            high, low = halves(arrived[pl.ds(half * 12 + f, groups, stride=24), :])
            at = pl.ds(f * groups, groups)
            table[0, at, half * LANES : (half + 1) * LANES] = high.astype(BF16)
            table[1, at, half * LANES : (half + 1) * LANES] = low.astype(BF16)
    for base in range(0, rows, width):
        slot = jnp.concatenate([slots[c : c + 1, :] for c in range(base, base + width)], axis=1)
        here = iota((groups, width * LANES), 0) == (slot >> 8)
        value = pick(table, slot_hot[:, base * LANES : (base + width) * LANES], here)
        for f in range(12):
            for number in range(width):
                at = f * rows + base + number
                found[at : at + 1, :] = value[f][:, number * LANES : (number + 1) * LANES]
    vector = [found[f * rows : (f + 1) * rows, :] for f in range(12)]
    terms = product_into(
        [None] * 12,
        lambda e: link_rows[e * rows : (e + 1) * rows, :],
        scale_rows[rows : 2 * rows, :],
        vector,
    )
    parts = [halves(term) for term in terms]
    bands = part.shape[1] // WIDE
    for c in range(rows):
        cell = cavity_index[c : c + 1, :]
        cols = slice(c * LANES, (c + 1) * LANES)
        band = cell >> 8
        zero = jnp.zeros((4, LANES), F32)
        tile = jnp.concatenate(
            [p[0][c : c + 1, :] for p in parts] + [zero] + [p[1][c : c + 1, :] for p in parts] + [zero],
            axis=0,
        )
        for b in range(bands):
            left[b * 32 : (b + 1) * 32, cols] = jnp.where(band == b, tile, 0.0).astype(BF16)
    added = lax.dot_general(
        left[...], cell_hot[...], (((1,), (1,)), ((), ())), preferred_element_type=F32
    )
    for b in range(bands):
        cols = slice(b * WIDE, (b + 1) * WIDE)
        out[:, cols] = part[:, cols] + (added[b * 32 : b * 32 + 12] + added[b * 32 + 16 : b * 32 + 28])


def exchange(values, sectors, features):
    chunks = values.shape[0] // features
    if sectors <= chunks:
        shaped = values.reshape(sectors, chunks // sectors * features, LANES)
        moved = lax.all_to_all(shaped, "circ", split_axis=0, concat_axis=0, tiled=True)
        return moved.reshape(values.shape)
    each = sectors // chunks
    shaped = values.reshape(chunks, features, each, LANES // each).transpose(0, 2, 1, 3)
    shaped = shaped.reshape(sectors, features, LANES // each)
    moved = lax.all_to_all(shaped, "circ", split_axis=0, concat_axis=0, tiled=True)
    moved = moved.reshape(chunks, each, features, LANES // each).transpose(0, 2, 1, 3)
    return moved.reshape(values.shape)


def on_device(
    seal_state,
    seal_blocks,
    seal_scales,
    seal_volume,
    cavity_state,
    cavity_blocks,
    cavity_scales,
    cavity_links,
    cavity_volume,
    link_owner,
    link_seal,
    link_cavity,
    link_blocks,
    link_scales,
):
    sectors = lax.axis_size("circ")
    segments = lax.axis_size("axial")
    _, seal_rows, _ = seal_state.shape
    cells = cavity_state.shape[1]
    count = link_seal.shape[0]
    rows = count // LANES
    groups = 2 * count // WIDE
    halo_rows = sectors * 2 == groups
    shape = jax.ShapeDtypeStruct
    owner = link_owner.reshape(rows, LANES)
    seal_index = link_seal.reshape(rows, LANES)
    cavity_index = link_cavity.reshape(rows, LANES)
    pair_blocks = link_blocks.transpose(1, 0, 2)

    hbm = lambda a: pltpu.with_memory_space_constraint(a, pltpu.HBM)
    head = (owner, seal_index, cavity_index, cavity_state, pair_blocks, link_scales)
    send, slots = pl.pallas_call(
        functools.partial(interface_kernel, sectors, halo_rows),
        in_specs=[HBM] * 7,
        out_specs=[VMEM, VMEM],
        out_shape=[shape((groups * 32, LANES), F32), shape((rows, LANES), I32)],
        scratch_shapes=[
            pltpu.VMEM((72 * rows, LANES), F32),
            pltpu.VMEM((2 * rows, LANES), F32),
            pltpu.VMEM((12 * cells // LANES, LANES), F32),
            pltpu.VMEM((26 * groups, count), BF16),
            pltpu.VMEM((WIDE, count), BF16),
        ]
        + [pltpu.VMEM(a.shape, a.dtype) for a in head]
        + [pltpu.VMEM((12, 8, LANES), F32)] * 2
        + [pltpu.SemaphoreType.DMA((8,))],
        compiler_params=PARAMS,
        name="interface",
    )(*[hbm(a) for a in head], hbm(seal_state))
    arrived = exchange(send, sectors, 16)

    faces, state, table = pl.pallas_call(
        face_kernel,
        in_specs=[HBM],
        out_specs=[VMEM] * 3,
        out_shape=[
            shape((seal_rows, LANES), F32),
            shape(seal_state.shape, F32),
            shape((2, 6 * seal_rows, WIDE), BF16),
        ],
        scratch_shapes=[pltpu.SemaphoreType.DMA((1,))],
        compiler_params=PARAMS,
        name="faces",
    )(hbm(seal_state))
    swaps = lambda begin: [
        pair for i in range(begin, segments - 1, 2) for pair in ((i, i + 1), (i + 1, i))
    ]
    inner = lax.ppermute(faces, "axial", swaps(0))
    outer = lax.ppermute(faces, "axial", swaps(1))
    if halo_rows:
        halos = ()
    else:
        first, last = seal_state[:, :1], seal_state[:, -1:]
        halos = (
            lax.ppermute(last, "circ", [(i, (i + 1) % sectors) for i in range(sectors)]),
            lax.ppermute(first, "circ", [((i + 1) % sectors, i) for i in range(sectors)]),
        )

    tile = (cavity_state, cavity_blocks, cavity_scales, cavity_links, cavity_volume.reshape(-1, LANES))
    tile = tile + (pair_blocks, link_scales)
    kept = (cavity_index, seal_blocks, seal_scales, seal_volume)
    cavity_part, link_rows, link_scale_rows, kept_index, kept_blocks, kept_scales, kept_volume = pl.pallas_call(
        cavity_kernel,
        in_specs=[HBM] * 11,
        out_specs=[VMEM] * 7,
        out_shape=[
            shape((12, cells), F32),
            shape((36 * rows, LANES), F32),
            shape((2 * rows, LANES), F32),
        ]
        + [shape(a.shape, a.dtype) for a in kept],
        scratch_shapes=[
            pltpu.VMEM((12 * cells // LANES, LANES), F32),
            pltpu.VMEM((180 * cells // LANES, LANES), F32),
            pltpu.VMEM((5 * cells // LANES, LANES), F32),
            pltpu.VMEM((4 * cells // LANES, LANES), I32),
            pltpu.VMEM((12 * cells // LANES, LANES), F32),
        ]
        + [pltpu.VMEM(a.shape, a.dtype) for a in tile]
        + [pltpu.SemaphoreType.DMA((11,))],
        compiler_params=PARAMS,
        cost_estimate=pl.CostEstimate(flops=10**6, bytes_accessed=10**7, transcendentals=0),
        name="cavity",
    )(*[hbm(a) for a in tile + kept])

    seal_part, edges = pl.pallas_call(
        functools.partial(seal_kernel, 16),
        in_specs=[VMEM] * 6,
        out_specs=[VMEM] * 2,
        out_shape=[shape(seal_state.shape, F32), shape((80, LANES), F32)],
        scratch_shapes=[
            pltpu.VMEM((2,) + seal_state.shape, F32),
            pltpu.VMEM((2,) + seal_state.shape, F32),
        ],
        compiler_params=PARAMS,
        cost_estimate=pl.CostEstimate(flops=10**6, bytes_accessed=10**7, transcendentals=0),
        name="seal",
    )(state, kept_blocks, kept_scales, kept_volume, inner, outer)

    arrived, seal_part, cavity_part = lax.optimization_barrier((arrived, seal_part, cavity_part))
    width = 8
    answers = pl.pallas_call(
        functools.partial(answer_kernel, width),
        in_specs=[VMEM] * 2,
        out_specs=HBM,
        out_shape=pltpu.HBM((groups * 24, LANES), F32),
        scratch_shapes=[
            pltpu.VMEM((groups * 24, LANES), F32),
            pltpu.SemaphoreType.DMA((2 * groups // width,)),
        ],
        compiler_params=PARAMS,
        name="answers",
    )(table, arrived)
    returned = exchange(answers, sectors, 12)

    deep = 4
    seal_result, slot_hot, cell_hot = pl.pallas_call(
        functools.partial(seal_add_kernel, halo_rows, sectors),
        in_specs=[VMEM] * (5 + len(halos)),
        out_specs=[VMEM] * 3,
        out_shape=[shape(seal_state.shape, F32)] + [shape((WIDE, count), BF16)] * 2,
        scratch_shapes=[
            pltpu.VMEM((12 * seal_rows, deep * LANES), BF16),
            pltpu.VMEM((WIDE, deep * LANES), BF16),
            pltpu.VMEM((12 * seal_rows, WIDE), F32),
        ],
        compiler_params=PARAMS,
        cost_estimate=pl.CostEstimate(flops=10**6, bytes_accessed=10**7, transcendentals=0),
        name="seal_add",
    )(seal_part, arrived, edges, slots, kept_index, *halos)

    cavity_result = pl.pallas_call(
        functools.partial(cavity_add_kernel, 8),
        in_specs=[VMEM] * 8,
        out_specs=VMEM,
        out_shape=shape((12, cells), F32),
        scratch_shapes=[
            pltpu.VMEM((32 * cells // WIDE, count), BF16),
            pltpu.VMEM((2, 12 * groups, WIDE), BF16),
            pltpu.VMEM((12 * rows, LANES), F32),
        ],
        compiler_params=PARAMS,
        name="cavity_add",
    )(cavity_part, returned, slots, kept_index, link_rows, link_scale_rows, slot_hot, cell_hot)
    return seal_result, cavity_result


def solution(mesh):
    return jax.shard_map(
        on_device,
        mesh=mesh,
        in_specs=(
            P(None, "circ", "axial"),
            P(None, None, "circ", "axial"),
            P(None, "circ", "axial"),
            P("circ", "axial"),
            P(None, ("circ", "axial")),
            P(None, None, ("circ", "axial")),
            P(None, ("circ", "axial")),
            P(None, ("circ", "axial")),
            P(("circ", "axial")),
            P(("circ", "axial"), None),
            P(("circ", "axial")),
            P(("circ", "axial")),
            P(None, None, ("circ", "axial")),
            P(None, ("circ", "axial")),
        ),
        out_specs=(P(None, "circ", "axial"), P(None, ("circ", "axial"))),
        check_vma=False,
    )
```

```python
import functools
import jax
import jax.numpy as jnp
from jax import lax
from jax.experimental import pallas as pl
from jax.experimental.pallas import tpu as pltpu
from jax.sharding import PartitionSpec as P

whirl_rate = 0.6
F32, BF16, I32, I16 = jnp.float32, jnp.bfloat16, jnp.int32, jnp.int16
LANES = 128
WIDE = 256
PARAMS = pltpu.CompilerParams(vmem_limit_bytes=16 * 1024 * 1024)
VMEM = pl.BlockSpec(memory_space=pltpu.VMEM)
HBM = pl.BlockSpec(memory_space=pltpu.HBM)


def iota(shape, axis):
    return lax.broadcasted_iota(I32, shape, axis)


def lane_take(row, index):
    table = jnp.broadcast_to(row, index.shape)
    return jnp.take_along_axis(table, index, axis=1, mode="promise_in_bounds")


def one_hot(index):
    return jnp.where(iota((WIDE, index.shape[1]), 0) == index, 1.0, 0.0).astype(BF16)


def halves(value):
    high = value.astype(BF16).astype(F32)
    return high, value - high


def coded(values):
    top = functools.reduce(jnp.maximum, [jnp.abs(v) for v in values])
    power = jnp.ceil(jnp.log2(jnp.maximum(top, 2.0**-100) * (1.0 / 32000.0)))
    factor = jnp.exp2(-power)
    return [jnp.round(v * factor) for v in values], power


def integer_halves(value):
    high = 256.0 * jnp.floor(value * (1.0 / 256.0))
    return high, value - high


def narrow(value):
    return value.astype(I32).astype(I16)


def widen(value):
    return value.astype(I32).astype(F32)


def chunk_base(chunk, block):
    return (chunk // 4) * block + (chunk % 4) * 16


def product_into(totals, entry, factor, vector):
    for row in range(6):
        real_part = imag_part = None
        for col in range(6):
            element = entry(6 * row + col)
            real_term, imag_term = element * vector[col], element * vector[6 + col]
            real_part = real_term if real_part is None else real_part + real_term
            imag_part = imag_term if imag_part is None else imag_part + imag_term
        real_part, imag_part = factor * real_part, factor * imag_part
        totals[row] = real_part if totals[row] is None else totals[row] + real_part
        totals[6 + row] = imag_part if totals[6 + row] is None else totals[6 + row] + imag_part
    return totals


def whirl(vector, volume):
    weight = whirl_rate * volume
    return [-weight * v for v in vector[6:]] + [weight * v for v in vector[:6]]


def fold_cells(source, target, count, base, cells):
    rows = cells // LANES
    for chunk in range(rows):
        target[pl.ds(base + chunk, count, stride=rows), :] = source[:, chunk * LANES : (chunk + 1) * LANES]


def interface_kernel(
    sectors, halo_rows, owner_hbm, seal_index_hbm, cavity_index_hbm, state_hbm, blocks_hbm,
    scales_hbm, seal_hbm, send, slots, seal, block_rows, scale_rows, state_rows, left, right,
    wide, owner, seal_index, cavity_index, state, blocks, scales, arrivals,
):
    loads = start_loads(
        (
            (owner_hbm, owner),
            (blocks_hbm, blocks),
            (scales_hbm, scales),
            (state_hbm, state),
            (cavity_index_hbm, cavity_index),
            (seal_index_hbm, seal_index),
            (seal_hbm, seal),
        ),
        arrivals,
    )
    loads[0].wait()
    rows = owner.shape[0]
    capacity = 2 * rows * LANES // sectors
    sector_id = iota((sectors, LANES), 0)
    hot = [
        jnp.where(sector_id == owner[c : c + 1, :], 1.0, 0.0).astype(F32) for c in range(rows)
    ]
    stacked = jnp.concatenate(hot, axis=0).astype(BF16)
    before = (iota((LANES, LANES), 0) < iota((LANES, LANES), 1)).astype(F32).astype(BF16)
    prefix = jnp.dot(stacked, before, preferred_element_type=F32)
    totals = jnp.dot(stacked, jnp.ones((LANES, LANES), BF16), preferred_element_type=F32)
    offset = jnp.zeros((sectors, LANES), F32)
    for c in range(rows):
        part = slice(c * sectors, (c + 1) * sectors)
        place = jnp.sum(hot[c] * (prefix[part] + offset), axis=0, keepdims=True)
        slots[c : c + 1, :] = owner[c : c + 1, :] * capacity + place.astype(I32)
        offset = offset + totals[part]
    for load in loads[1:-1]:
        load.wait()
    for entry in range(36):
        both = blocks[entry].astype(F32)
        for c in range(rows):
            block_rows[pl.ds(entry * rows + c, 2, stride=36 * rows), :] = both[
                :, c * LANES : (c + 1) * LANES
            ]
    fold_cells(scales, scale_rows, 2, 0, rows * LANES)
    fold_cells(state, state_rows, 12, 0, state.shape[1])
    tile_rows = state.shape[1] // LANES
    cell = cavity_index[...]
    lane, high = cell & (LANES - 1), cell >> 7
    vector = [jnp.zeros((rows, LANES), F32)] * 12
    for r in range(tile_rows):
        here = high == r
        for f in range(12):
            row = state_rows[f * tile_rows + r : f * tile_rows + r + 1, :]
            vector[f] = jnp.where(here, lane_take(row, lane), vector[f])
    terms = product_into(
        [None] * 12, lambda e: block_rows[e * rows : (e + 1) * rows, :], scale_rows[0:rows, :], vector
    )
    terms, power = coded(terms)
    terms = terms + [seal_index[...].astype(F32), power]
    parts = [half for term in terms for half in integer_halves(term)]
    groups = 2 * rows * LANES // WIDE
    for c in range(rows):
        slot = slots[c : c + 1, :]
        cols = slice(c * LANES, (c + 1) * LANES)
        right[:, cols] = one_hot(slot & (WIDE - 1))
        here = iota((groups, LANES), 0) == (slot >> 8)
        for number, part in enumerate(parts):
            left[number * groups : (number + 1) * groups, cols] = jnp.where(
                here, part[c : c + 1, :], 0.0
            ).astype(BF16)
    moved = lax.dot_general(
        left[...], right[...], (((1,), (1,)), ((), ())), preferred_element_type=F32
    )
    for number in range(14):
        pair = moved[2 * number * groups : (2 * number + 2) * groups]
        value = pair[:groups] + pair[groups:]
        for half in range(2):
            wide[pl.ds(half * 16 + number, groups, stride=32), :] = value[
                :, half * LANES : (half + 1) * LANES
            ]
    for number in range(14, 16):
        wide[pl.ds(number, 2 * groups, stride=16), :] = jnp.zeros((2 * groups, LANES), F32)
    loads[-1].wait()
    block = send.shape[0] * 2 // groups
    for at in range(0, groups // 2):
        send[at * block : at * block + 64, :] = narrow(wide[at * 64 : at * 64 + 64, :])
    if halo_rows:
        me = lax.axis_index("circ")
        zero = jnp.zeros((16, LANES), I16)
        for at in range(0, groups // 2):
            send[at * block + 64 : at * block + 80, :] = zero
        for step, row in ((1, seal.shape[1] - 1), (sectors - 1, 0)):
            base = pl.multiple_of(lax.rem(me + step, sectors) * block + 64, 16)
            values, power = coded([seal[f, row : row + 1, :] for f in range(12)])
            tile = jnp.concatenate(values + [power] + [jnp.zeros((3, LANES), F32)], axis=0)
            send[pl.ds(base, 16), :] = narrow(tile)


def start_loads(pairs, arrivals):
    loads = [
        pltpu.make_async_copy(source, target, arrivals.at[number])
        for number, (source, target) in enumerate(pairs)
    ]
    for load in loads:
        load.start()
    return loads


def face_kernel(state, faces, table):
    lane = iota(faces.shape, 1)
    half_rows = faces.shape[0] // 2
    total = jnp.zeros(faces.shape, F32)
    for f in range(12):
        total = jnp.where(lane == f, pltpu.roll(state[f], f + 1, 1), total)
        total = jnp.where(lane == 16 + f, pltpu.roll(state[f], 16 + f, 1), total)
    faces[...] = total
    for half in range(2):
        here = slice(half * half_rows, (half + 1) * half_rows)
        values, power = coded([state[f, here, :] for f in range(12)])
        for f, value in enumerate(values + [power]):
            high, low = integer_halves(value)
            at = pl.ds(f * half_rows, half_rows)
            table[at, half * LANES : (half + 1) * LANES] = high.astype(BF16)
            table[at, WIDE + half * LANES : WIDE + (half + 1) * LANES] = low.astype(BF16)


def seal_kernel(step_rows, state, blocks, scales, volume, out, edges, beside, along):
    rows = state.shape[1]
    lane = iota((rows, LANES), 1)
    for f in range(12):
        beside[0, f, 1:rows, :] = state[f, 0 : rows - 1, :]
        beside[0, f, 0:1, :] = jnp.zeros((1, LANES), F32)
        beside[1, f, 0 : rows - 1, :] = state[f, 1:rows, :]
        beside[1, f, rows - 1 : rows, :] = jnp.zeros((1, LANES), F32)
        own = state[f]
        along[0, f] = jnp.where(lane == 0, 0.0, pltpu.roll(own, 1, 1))
        along[1, f] = jnp.where(lane == LANES - 1, 0.0, pltpu.roll(own, LANES - 1, 1))

    def add_rows(step, carry):
        here = pl.ds(pl.multiple_of(step * step_rows, step_rows), step_rows)
        own = [state[f, here, :] for f in range(12)]
        totals = whirl(own, volume[here, :])
        for number in range(5):
            if number == 0:
                vector = own
            else:
                source = beside if number < 3 else along
                vector = [source[(number - 1) % 2, f, here, :] for f in range(12)]
            totals = product_into(
                totals, lambda e: blocks[number, e, here, :].astype(F32), scales[number, here, :], vector
            )
        for f in range(12):
            out[f, here, :] = totals[f]
        return carry

    lax.fori_loop(0, rows // step_rows, add_rows, 0)
    for number, near, at in ((1, 0, 0), (2, rows - 16, 15)):
        first = (number - 1) * 40
        for e in range(36):
            tile = blocks[number, e, near : near + 16, :].astype(F32)
            edges[first + e : first + e + 1, :] = tile[at : at + 1, :]
        edges[first + 36 : first + 37, :] = scales[number, near + at : near + at + 1, :]
        edges[first + 37 : first + 40, :] = jnp.zeros((3, LANES), F32)


def end_columns_kernel(step_rows, part, blocks, scales, inner, outer, out):
    odd = lax.rem(lax.axis_index("axial"), 2) == 1

    def add_rows(step, carry):
        here = pl.ds(pl.multiple_of(step * step_rows, step_rows), step_rows)
        first, second = inner[here, :], outer[here, :]
        low, high = jnp.where(odd, first, second), jnp.where(odd, second, first)
        lane = iota((step_rows, LANES), 1)
        left_half = lane < LANES // 2
        vector = []
        for f in range(12):
            left = pltpu.roll(low, (LANES - f) % LANES, 1)
            right = pltpu.roll(high, LANES - 1 - 16 - f, 1)
            vector.append(jnp.where(lane == 0, left, jnp.where(lane == LANES - 1, right, 0.0)))
        totals = product_into(
            [part[f, here, :] for f in range(12)],
            lambda e: jnp.where(
                left_half, blocks[3, e, here, :].astype(F32), blocks[4, e, here, :].astype(F32)
            ),
            jnp.where(left_half, scales[3, here, :], scales[4, here, :]),
            vector,
        )
        for f in range(12):
            out[f, here, :] = totals[f]
        return carry

    lax.fori_loop(0, part.shape[1] // step_rows, add_rows, 0)


def pick(table, hot, here):
    found = jnp.dot(table[...], jnp.concatenate([hot, hot], axis=0), preferred_element_type=F32)
    bands = here.shape[0]
    return [
        jnp.sum(jnp.where(here, found[f * bands : (f + 1) * bands, :], 0.0), axis=0, keepdims=True)
        for f in range(table.shape[0] // bands)
    ]


def answer_kernel(width, block, table, arrived, send_hbm, wide, send, sent):
    chunks = wide.shape[0] // 16
    half_rows = table.shape[0] // 13
    copies = []
    for number in range(13, 16):
        wide[pl.ds(number, chunks, stride=16), :] = jnp.zeros((chunks, LANES), F32)
    for base in range(0, chunks, width):
        cell = []
        for g in range(base, base + width):
            at = chunk_base(g, block)
            cell.append(arrived[at : at + 16, :].astype(I32)[12:13, :])
        cell = jnp.concatenate(cell, axis=1)
        row = cell >> 7
        upper = row >= half_rows
        index = (cell & (LANES - 1)) + jnp.where(upper, LANES, 0)
        row = row - jnp.where(upper, half_rows, 0)
        here = iota((half_rows, width * LANES), 0) == row
        value = pick(table, one_hot(index), here)
        for f in range(13):
            for part in range(width):
                at = (base + part) * 16 + f
                wide[at : at + 1, :] = value[f][:, part * LANES : (part + 1) * LANES]
        done = pl.ds(base * 16, width * 16)
        send[done, :] = narrow(wide[done, :])
        copies.append(
            pltpu.make_async_copy(send.at[done, :], send_hbm.at[done, :], sent.at[base // width])
        )
        copies[-1].start()
    for copy in copies:
        copy.wait()


def seal_add_kernel(
    halo_rows, sectors, block, part, arrived, edges, slots, cavity_index,
    *refs,
):
    *halos, out, slot_hot, cell_hot, left, right, total = refs
    chunks = arrived.shape[0] // block * 4
    rows = part.shape[1]
    half_rows = rows // 2
    total[...] = jnp.zeros_like(total)
    deep = left.shape[1] // LANES

    def add_chunks(step, carry):
        for sub in range(deep):
            base = pl.multiple_of(step * (deep // 4 * block) + chunk_base(sub, block), 16)
            tile = arrived[pl.ds(base, 16), :].astype(I32)
            cell = tile[12:13, :]
            tile = tile.astype(F32)
            high, low = halves(tile * jnp.exp2(tile[13:14, :]))
            row = cell >> 7
            column = (cell & (LANES - 1)) + jnp.where(row >= half_rows, LANES, 0)
            row = jnp.where(row >= half_rows, row - half_rows, row)
            cols = slice(sub * LANES, (sub + 1) * LANES)
            right[:, cols] = one_hot(column)
            here = iota((half_rows, LANES), 0) == row
            for f in range(12):
                for number, source in enumerate((high, low)):
                    at = (2 * f + number) * half_rows
                    left[at : at + half_rows, cols] = jnp.where(
                        here, source[f : f + 1, :], 0.0
                    ).astype(BF16)
        total[...] += lax.dot_general(
            left[...], right[...], (((1,), (1,)), ((), ())), preferred_element_type=F32
        )
        return carry

    for c in range(slots.shape[0]):
        cols = slice(c * LANES, (c + 1) * LANES)
        for source, target in ((slots, slot_hot), (cavity_index, cell_hot)):
            target[:, cols] = one_hot(source[c : c + 1, :] & (WIDE - 1))
    lax.fori_loop(0, chunks // deep, add_chunks, 0)
    for f in range(12):
        added = (
            total[2 * f * half_rows : (2 * f + 1) * half_rows, :]
            + total[(2 * f + 1) * half_rows : (2 * f + 2) * half_rows, :]
        )
        out[f, 0:half_rows, :] = part[f, 0:half_rows, :] + added[:, :LANES]
        out[f, half_rows:rows, :] = part[f, half_rows:rows, :] + added[:, LANES:]
    me = lax.axis_index("circ")
    for number, step in ((1, sectors - 1), (2, 1)):
        if halo_rows:
            base = pl.multiple_of(lax.rem(me + step, sectors) * block + 64, 16)
            tile = widen(arrived[pl.ds(base, 16), :])
            tile = tile * jnp.exp2(tile[12:13, :])
            vector = [tile[f : f + 1, :] for f in range(12)]
        else:
            vector = [halos[number - 1][f] for f in range(12)]
        at = 0 if number == 1 else rows - 1
        first = (number - 1) * 40
        terms = product_into(
            [None] * 12,
            lambda e: edges[first + e : first + e + 1, :],
            edges[first + 36 : first + 37, :],
            vector,
        )
        for f in range(12):
            out[f, at : at + 1, :] = out[f, at : at + 1, :] + terms[f]


def cavity_kernel(
    state_hbm, blocks_hbm, scales_hbm, links_hbm, volume_hbm, link_blocks_hbm, link_scales_hbm,
    index_hbm, seal_blocks_hbm, seal_scales_hbm, seal_volume_hbm,
    out, link_rows, link_scale_rows, cavity_index, seal_blocks, seal_scales, seal_volume,
    state_rows, block_rows, scale_rows, face_rows, out_rows,
    state, blocks, scales, links, volume, link_blocks, link_scales, arrivals,
):
    loads = start_loads(
        (
            (state_hbm, state),
            (links_hbm, links),
            (blocks_hbm, blocks),
            (scales_hbm, scales),
            (volume_hbm, volume),
            (link_blocks_hbm, link_blocks),
            (link_scales_hbm, link_scales),
            (index_hbm, cavity_index),
            (seal_scales_hbm, seal_scales),
            (seal_volume_hbm, seal_volume),
            (seal_blocks_hbm, seal_blocks),
        ),
        arrivals,
    )
    for load in loads[:7]:
        load.wait()
    cells = state.shape[1]
    rows = cells // LANES
    fold_cells(state, state_rows, 12, 0, cells)
    fold_cells(scales, scale_rows, 5, 0, cells)
    fold_cells(links, face_rows, 4, 0, cells)
    for number in range(5):
        for c in range(rows):
            block_rows[pl.ds(number * 36 * rows + c, 36, stride=rows), :] = blocks[
                number, :, c * LANES : (c + 1) * LANES
            ].astype(F32)
    own = [state_rows[f * rows : (f + 1) * rows, :] for f in range(12)]
    totals = whirl(own, volume[...])
    for number in range(5):
        if number == 0:
            vector = own
        else:
            cell = face_rows[(number - 1) * rows : number * rows, :]
            lane, high = cell & (LANES - 1), cell >> 7
            vector = [jnp.zeros((rows, LANES), F32)] * 12
            for r in range(rows):
                here = high == r
                for f in range(12):
                    row = state_rows[f * rows + r : f * rows + r + 1, :]
                    vector[f] = jnp.where(here, lane_take(row, lane), vector[f])
        base = number * 36 * rows
        totals = product_into(
            totals,
            lambda e: block_rows[base + e * rows : base + (e + 1) * rows, :],
            scale_rows[number * rows : (number + 1) * rows, :],
            vector,
        )
    for f in range(12):
        out_rows[f * rows : (f + 1) * rows, :] = totals[f]
    for c in range(rows):
        out[:, c * LANES : (c + 1) * LANES] = out_rows[pl.ds(c, 12, stride=rows), :]
    row_count = link_blocks.shape[2] // LANES
    for entry in range(36):
        both = link_blocks[entry].astype(F32)
        for c in range(row_count):
            link_rows[entry * row_count + c : entry * row_count + c + 1, :] = both[
                1:2, c * LANES : (c + 1) * LANES
            ]
    fold_cells(link_scales, link_scale_rows, 2, 0, row_count * LANES)
    for load in loads[7:]:
        load.wait()


def cavity_add_kernel(
    width, part, arrived, slots, cavity_index, link_rows, scale_rows, slot_hot, cell_hot,
    out, left, table, found, wide,
):
    rows = slots.shape[0]
    chunks = arrived.shape[0] // 16
    groups = chunks // 2
    wide[...] = widen(arrived[...])
    for half in range(2):
        factor = jnp.exp2(wide[pl.ds(half * 16 + 12, groups, stride=32), :])
        for f in range(12):
            high, low = halves(wide[pl.ds(half * 16 + f, groups, stride=32), :] * factor)
            at = pl.ds(f * groups, groups)
            table[at, half * LANES : (half + 1) * LANES] = high.astype(BF16)
            table[at, WIDE + half * LANES : WIDE + (half + 1) * LANES] = low.astype(BF16)
    for base in range(0, rows, width):
        slot = jnp.concatenate([slots[c : c + 1, :] for c in range(base, base + width)], axis=1)
        here = iota((groups, width * LANES), 0) == (slot >> 8)
        value = pick(table, slot_hot[:, base * LANES : (base + width) * LANES], here)
        for f in range(12):
            for number in range(width):
                at = f * rows + base + number
                found[at : at + 1, :] = value[f][:, number * LANES : (number + 1) * LANES]
    vector = [found[f * rows : (f + 1) * rows, :] for f in range(12)]
    terms = product_into(
        [None] * 12,
        lambda e: link_rows[e * rows : (e + 1) * rows, :],
        scale_rows[rows : 2 * rows, :],
        vector,
    )
    parts = [halves(term) for term in terms]
    bands = part.shape[1] // WIDE
    for c in range(rows):
        cell = cavity_index[c : c + 1, :]
        cols = slice(c * LANES, (c + 1) * LANES)
        band = cell >> 8
        zero = jnp.zeros((4, LANES), F32)
        tile = jnp.concatenate(
            [p[0][c : c + 1, :] for p in parts] + [zero] + [p[1][c : c + 1, :] for p in parts] + [zero],
            axis=0,
        )
        for b in range(bands):
            left[b * 32 : (b + 1) * 32, cols] = jnp.where(band == b, tile, 0.0).astype(BF16)
    added = lax.dot_general(
        left[...], cell_hot[...], (((1,), (1,)), ((), ())), preferred_element_type=F32
    )
    for b in range(bands):
        cols = slice(b * WIDE, (b + 1) * WIDE)
        out[:, cols] = part[:, cols] + (added[b * 32 : b * 32 + 12] + added[b * 32 + 16 : b * 32 + 28])


def exchange(values, sectors, chunks):
    if sectors <= chunks:
        shaped = values.reshape(sectors, -1, LANES)
        moved = lax.all_to_all(shaped, "circ", split_axis=0, concat_axis=0, tiled=True)
        return moved.reshape(values.shape)
    each = sectors // chunks
    shaped = values.reshape(chunks, 16, each, LANES // each).transpose(0, 2, 1, 3)
    shaped = shaped.reshape(sectors, 16, LANES // each)
    moved = lax.all_to_all(shaped, "circ", split_axis=0, concat_axis=0, tiled=True)
    moved = moved.reshape(chunks, each, 16, LANES // each).transpose(0, 2, 1, 3)
    return moved.reshape(values.shape)


def on_device(
    seal_state,
    seal_blocks,
    seal_scales,
    seal_volume,
    cavity_state,
    cavity_blocks,
    cavity_scales,
    cavity_links,
    cavity_volume,
    link_owner,
    link_seal,
    link_cavity,
    link_blocks,
    link_scales,
):
    sectors = lax.axis_size("circ")
    segments = lax.axis_size("axial")
    _, seal_rows, _ = seal_state.shape
    cells = cavity_state.shape[1]
    count = link_seal.shape[0]
    rows = count // LANES
    groups = 2 * count // WIDE
    halo_rows = sectors * 2 == groups
    shape = jax.ShapeDtypeStruct
    owner = link_owner.reshape(rows, LANES)
    seal_index = link_seal.reshape(rows, LANES)
    cavity_index = link_cavity.reshape(rows, LANES)
    pair_blocks = link_blocks.transpose(1, 0, 2)

    hbm = lambda a: pltpu.with_memory_space_constraint(a, pltpu.HBM)
    head = (owner, seal_index, cavity_index, cavity_state, pair_blocks, link_scales)
    block = 80 if halo_rows else 64
    send, slots, state = pl.pallas_call(
        functools.partial(interface_kernel, sectors, halo_rows),
        in_specs=[HBM] * 7,
        out_specs=[VMEM] * 3,
        out_shape=[
            shape((groups // 2 * block, LANES), I16),
            shape((rows, LANES), I32),
            shape(seal_state.shape, F32),
        ],
        scratch_shapes=[
            pltpu.VMEM((72 * rows, LANES), F32),
            pltpu.VMEM((2 * rows, LANES), F32),
            pltpu.VMEM((12 * cells // LANES, LANES), F32),
            pltpu.VMEM((28 * groups, count), BF16),
            pltpu.VMEM((WIDE, count), BF16),
            pltpu.VMEM((groups * 32, LANES), F32),
        ]
        + [pltpu.VMEM(a.shape, a.dtype) for a in head]
        + [pltpu.SemaphoreType.DMA((7,))],
        compiler_params=PARAMS,
        name="interface",
    )(*[hbm(a) for a in head], hbm(seal_state))
    arrived = exchange(send, sectors, 2 * groups)

    faces, table = pl.pallas_call(
        face_kernel,
        in_specs=[VMEM],
        out_specs=[VMEM] * 2,
        out_shape=[
            shape((seal_rows, LANES), F32),
            shape((13 * seal_rows // 2, 2 * WIDE), BF16),
        ],
        compiler_params=PARAMS,
        name="faces",
    )(state)
    swaps = lambda begin: [
        pair for i in range(begin, segments - 1, 2) for pair in ((i, i + 1), (i + 1, i))
    ]
    inner = lax.ppermute(faces, "axial", swaps(0))
    outer = lax.ppermute(faces, "axial", swaps(1))
    if halo_rows:
        halos = ()
    else:
        first, last = seal_state[:, :1], seal_state[:, -1:]
        halos = (
            lax.ppermute(last, "circ", [(i, (i + 1) % sectors) for i in range(sectors)]),
            lax.ppermute(first, "circ", [((i + 1) % sectors, i) for i in range(sectors)]),
        )

    tile = (cavity_state, cavity_blocks, cavity_scales, cavity_links, cavity_volume.reshape(-1, LANES))
    tile = tile + (pair_blocks, link_scales)
    kept = (cavity_index, seal_blocks, seal_scales, seal_volume)
    cavity_part, link_rows, link_scale_rows, kept_index, kept_blocks, kept_scales, kept_volume = pl.pallas_call(
        cavity_kernel,
        in_specs=[HBM] * 11,
        out_specs=[VMEM] * 7,
        out_shape=[
            shape((12, cells), F32),
            shape((36 * rows, LANES), F32),
            shape((2 * rows, LANES), F32),
        ]
        + [shape(a.shape, a.dtype) for a in kept],
        scratch_shapes=[
            pltpu.VMEM((12 * cells // LANES, LANES), F32),
            pltpu.VMEM((180 * cells // LANES, LANES), F32),
            pltpu.VMEM((5 * cells // LANES, LANES), F32),
            pltpu.VMEM((4 * cells // LANES, LANES), I32),
            pltpu.VMEM((12 * cells // LANES, LANES), F32),
        ]
        + [pltpu.VMEM(a.shape, a.dtype) for a in tile]
        + [pltpu.SemaphoreType.DMA((11,))],
        compiler_params=PARAMS,
        cost_estimate=pl.CostEstimate(flops=10**6, bytes_accessed=10**7, transcendentals=0),
        name="cavity",
    )(*[hbm(a) for a in tile + kept])

    seal_part, edges = pl.pallas_call(
        functools.partial(seal_kernel, 16),
        in_specs=[VMEM] * 4,
        out_specs=[VMEM] * 2,
        out_shape=[shape(seal_state.shape, F32), shape((80, LANES), F32)],
        scratch_shapes=[
            pltpu.VMEM((2,) + seal_state.shape, F32),
            pltpu.VMEM((2,) + seal_state.shape, F32),
        ],
        compiler_params=PARAMS,
        cost_estimate=pl.CostEstimate(flops=10**6, bytes_accessed=10**7, transcendentals=0),
        name="seal",
    )(state, kept_blocks, kept_scales, kept_volume)
    seal_part = pl.pallas_call(
        functools.partial(end_columns_kernel, 16),
        in_specs=[VMEM] * 5,
        out_specs=VMEM,
        out_shape=shape(seal_state.shape, F32),
        compiler_params=PARAMS,
        name="end_columns",
    )(seal_part, kept_blocks, kept_scales, inner, outer)

    arrived, seal_part, cavity_part = lax.optimization_barrier((arrived, seal_part, cavity_part))
    width = 8
    answers = pl.pallas_call(
        functools.partial(answer_kernel, width, block),
        in_specs=[VMEM] * 2,
        out_specs=HBM,
        out_shape=pltpu.HBM((groups * 32, LANES), I16),
        scratch_shapes=[
            pltpu.VMEM((groups * 32, LANES), F32),
            pltpu.VMEM((groups * 32, LANES), I16),
            pltpu.SemaphoreType.DMA((2 * groups // width,)),
        ],
        compiler_params=PARAMS,
        name="answers",
    )(table, arrived)
    returned = exchange(answers, sectors, 2 * groups)

    deep = 8
    seal_result, slot_hot, cell_hot = pl.pallas_call(
        functools.partial(seal_add_kernel, halo_rows, sectors, block),
        in_specs=[VMEM] * (5 + len(halos)),
        out_specs=[VMEM] * 3,
        out_shape=[shape(seal_state.shape, F32)] + [shape((WIDE, count), BF16)] * 2,
        scratch_shapes=[
            pltpu.VMEM((12 * seal_rows, deep * LANES), BF16),
            pltpu.VMEM((WIDE, deep * LANES), BF16),
            pltpu.VMEM((12 * seal_rows, WIDE), F32),
        ],
        compiler_params=PARAMS,
        cost_estimate=pl.CostEstimate(flops=10**6, bytes_accessed=10**7, transcendentals=0),
        name="seal_add",
    )(seal_part, arrived, edges, slots, kept_index, *halos)

    cavity_result = pl.pallas_call(
        functools.partial(cavity_add_kernel, 8),
        in_specs=[VMEM] * 8,
        out_specs=VMEM,
        out_shape=shape((12, cells), F32),
        scratch_shapes=[
            pltpu.VMEM((32 * cells // WIDE, count), BF16),
            pltpu.VMEM((12 * groups, 2 * WIDE), BF16),
            pltpu.VMEM((12 * rows, LANES), F32),
            pltpu.VMEM((groups * 32, LANES), F32),
        ],
        compiler_params=PARAMS,
        name="cavity_add",
    )(cavity_part, returned, slots, kept_index, link_rows, link_scale_rows, slot_hot, cell_hot)
    return seal_result, cavity_result


def solution(mesh):
    return jax.shard_map(
        on_device,
        mesh=mesh,
        in_specs=(
            P(None, "circ", "axial"),
            P(None, None, "circ", "axial"),
            P(None, "circ", "axial"),
            P("circ", "axial"),
            P(None, ("circ", "axial")),
            P(None, None, ("circ", "axial")),
            P(None, ("circ", "axial")),
            P(None, ("circ", "axial")),
            P(("circ", "axial")),
            P(("circ", "axial"), None),
            P(("circ", "axial")),
            P(("circ", "axial")),
            P(None, None, ("circ", "axial")),
            P(None, ("circ", "axial")),
        ),
        out_specs=(P(None, "circ", "axial"), P(None, ("circ", "axial"))),
        check_vma=False,
    )
```

```python
import functools
import jax
import jax.numpy as jnp
from jax import lax
from jax.experimental import pallas as pl
from jax.experimental.pallas import tpu as pltpu
from jax.sharding import PartitionSpec as P

whirl_rate = 0.6
F32, BF16, I32, I16 = jnp.float32, jnp.bfloat16, jnp.int32, jnp.int16
LANES = 128
WIDE = 256
PARAMS = pltpu.CompilerParams(vmem_limit_bytes=16 * 1024 * 1024)
VMEM = pl.BlockSpec(memory_space=pltpu.VMEM)
HBM = pl.BlockSpec(memory_space=pltpu.HBM)


def iota(shape, axis):
    return lax.broadcasted_iota(I32, shape, axis)


def lane_take(row, index):
    table = jnp.broadcast_to(row, index.shape)
    return jnp.take_along_axis(table, index, axis=1, mode="promise_in_bounds")


def one_hot(index):
    return jnp.where(iota((WIDE, index.shape[1]), 0) == index, 1.0, 0.0).astype(BF16)


def halves(value):
    high = value.astype(BF16).astype(F32)
    return high, value - high


def coded(values):
    top = functools.reduce(jnp.maximum, [jnp.abs(v) for v in values])
    power = jnp.ceil(jnp.log2(jnp.maximum(top, 2.0**-100) * (1.0 / 32000.0)))
    factor = jnp.exp2(-power)
    return [jnp.round(v * factor) for v in values], power


def integer_halves(value):
    high = 256.0 * jnp.floor(value * (1.0 / 256.0))
    return high, value - high


def narrow(value):
    return value.astype(I32).astype(I16)


def widen(value):
    return value.astype(I32).astype(F32)


def chunk_base(chunk, block):
    return (chunk // 4) * block + (chunk % 4) * 16


def product_into(totals, entry, factor, vector):
    for row in range(6):
        real_part = imag_part = None
        for col in range(6):
            element = entry(6 * row + col)
            real_term, imag_term = element * vector[col], element * vector[6 + col]
            real_part = real_term if real_part is None else real_part + real_term
            imag_part = imag_term if imag_part is None else imag_part + imag_term
        real_part, imag_part = factor * real_part, factor * imag_part
        totals[row] = real_part if totals[row] is None else totals[row] + real_part
        totals[6 + row] = imag_part if totals[6 + row] is None else totals[6 + row] + imag_part
    return totals


def whirl(vector, volume):
    weight = whirl_rate * volume
    return [-weight * v for v in vector[6:]] + [weight * v for v in vector[:6]]


def fold_cells(source, target, count, base, cells):
    rows = cells // LANES
    for chunk in range(rows):
        target[pl.ds(base + chunk, count, stride=rows), :] = source[:, chunk * LANES : (chunk + 1) * LANES]


def interface_kernel(
    sectors, halo_rows, owner_hbm, seal_index_hbm, cavity_index_hbm, state_hbm, blocks_hbm,
    scales_hbm, seal_hbm, tile_blocks_hbm, tile_scales_hbm, tile_links_hbm, tile_volume_hbm,
    send, slots, seal, cavity_index, state, tile_blocks, tile_scales, tile_links, tile_volume,
    block_rows, scale_rows, state_rows, left, right, wide, owner, seal_index, blocks, scales,
    arrivals,
):
    loads = start_loads(
        (
            (owner_hbm, owner),
            (blocks_hbm, blocks),
            (scales_hbm, scales),
            (state_hbm, state),
            (cavity_index_hbm, cavity_index),
            (seal_index_hbm, seal_index),
            (seal_hbm, seal),
            (tile_blocks_hbm, tile_blocks),
            (tile_scales_hbm, tile_scales),
            (tile_links_hbm, tile_links),
            (tile_volume_hbm, tile_volume),
        ),
        arrivals,
    )
    loads[0].wait()
    rows = owner.shape[0]
    capacity = 2 * rows * LANES // sectors
    sector_id = iota((sectors, LANES), 0)
    hot = [
        jnp.where(sector_id == owner[c : c + 1, :], 1.0, 0.0).astype(F32) for c in range(rows)
    ]
    stacked = jnp.concatenate(hot, axis=0).astype(BF16)
    before = (iota((LANES, LANES), 0) < iota((LANES, LANES), 1)).astype(F32).astype(BF16)
    prefix = jnp.dot(stacked, before, preferred_element_type=F32)
    totals = jnp.dot(stacked, jnp.ones((LANES, LANES), BF16), preferred_element_type=F32)
    offset = jnp.zeros((sectors, LANES), F32)
    for c in range(rows):
        part = slice(c * sectors, (c + 1) * sectors)
        place = jnp.sum(hot[c] * (prefix[part] + offset), axis=0, keepdims=True)
        slots[c : c + 1, :] = owner[c : c + 1, :] * capacity + place.astype(I32)
        offset = offset + totals[part]
    for load in loads[1:6]:
        load.wait()
    for entry in range(36):
        both = blocks[entry].astype(F32)
        for c in range(rows):
            block_rows[pl.ds(entry * rows + c, 2, stride=36 * rows), :] = both[
                :, c * LANES : (c + 1) * LANES
            ]
    fold_cells(scales, scale_rows, 2, 0, rows * LANES)
    fold_cells(state, state_rows, 12, 0, state.shape[1])
    tile_rows = state.shape[1] // LANES
    cell = cavity_index[...]
    lane, high = cell & (LANES - 1), cell >> 7
    vector = [jnp.zeros((rows, LANES), F32)] * 12
    for r in range(tile_rows):
        here = high == r
        for f in range(12):
            row = state_rows[f * tile_rows + r : f * tile_rows + r + 1, :]
            vector[f] = jnp.where(here, lane_take(row, lane), vector[f])
    terms = product_into(
        [None] * 12, lambda e: block_rows[e * rows : (e + 1) * rows, :], scale_rows[0:rows, :], vector
    )
    terms, power = coded(terms)
    terms = terms + [seal_index[...].astype(F32), power]
    parts = [half for term in terms for half in integer_halves(term)]
    groups = 2 * rows * LANES // WIDE
    for c in range(rows):
        slot = slots[c : c + 1, :]
        cols = slice(c * LANES, (c + 1) * LANES)
        right[:, cols] = one_hot(slot & (WIDE - 1))
        here = iota((groups, LANES), 0) == (slot >> 8)
        for number, part in enumerate(parts):
            left[number * groups : (number + 1) * groups, cols] = jnp.where(
                here, part[c : c + 1, :], 0.0
            ).astype(BF16)
    moved = lax.dot_general(
        left[...], right[...], (((1,), (1,)), ((), ())), preferred_element_type=F32
    )
    for number in range(14):
        pair = moved[2 * number * groups : (2 * number + 2) * groups]
        value = pair[:groups] + pair[groups:]
        for half in range(2):
            wide[pl.ds(half * 16 + number, groups, stride=32), :] = value[
                :, half * LANES : (half + 1) * LANES
            ]
    for number in range(14, 16):
        wide[pl.ds(number, 2 * groups, stride=16), :] = jnp.zeros((2 * groups, LANES), F32)
    for load in loads[6:]:
        load.wait()
    block = send.shape[0] * 2 // groups
    for at in range(0, groups // 2):
        send[at * block : at * block + 64, :] = narrow(wide[at * 64 : at * 64 + 64, :])
    if halo_rows:
        me = lax.axis_index("circ")
        zero = jnp.zeros((16, LANES), I16)
        for at in range(0, groups // 2):
            send[at * block + 64 : at * block + 80, :] = zero
        for step, row in ((1, seal.shape[1] - 1), (sectors - 1, 0)):
            base = pl.multiple_of(lax.rem(me + step, sectors) * block + 64, 16)
            values, power = coded([seal[f, row : row + 1, :] for f in range(12)])
            tile = jnp.concatenate(values + [power] + [jnp.zeros((3, LANES), F32)], axis=0)
            send[pl.ds(base, 16), :] = narrow(tile)


def start_loads(pairs, arrivals):
    loads = [
        pltpu.make_async_copy(source, target, arrivals.at[number])
        for number, (source, target) in enumerate(pairs)
    ]
    for load in loads:
        load.start()
    return loads


def face_kernel(state, faces, table):
    lane = iota(faces.shape, 1)
    half_rows = faces.shape[0] // 2
    total = jnp.zeros(faces.shape, F32)
    for f in range(12):
        total = jnp.where(lane == f, pltpu.roll(state[f], f + 1, 1), total)
        total = jnp.where(lane == 16 + f, pltpu.roll(state[f], 16 + f, 1), total)
    faces[...] = total
    for half in range(2):
        here = slice(half * half_rows, (half + 1) * half_rows)
        values, power = coded([state[f, here, :] for f in range(12)])
        for f, value in enumerate(values + [power]):
            high, low = integer_halves(value)
            at = pl.ds(f * half_rows, half_rows)
            table[at, half * LANES : (half + 1) * LANES] = high.astype(BF16)
            table[at, WIDE + half * LANES : WIDE + (half + 1) * LANES] = low.astype(BF16)


def seal_kernel(step_rows, state, blocks, scales, volume, out, edges, beside, along):
    rows = state.shape[1]
    lane = iota((rows, LANES), 1)
    for f in range(12):
        beside[0, f, 1:rows, :] = state[f, 0 : rows - 1, :]
        beside[0, f, 0:1, :] = jnp.zeros((1, LANES), F32)
        beside[1, f, 0 : rows - 1, :] = state[f, 1:rows, :]
        beside[1, f, rows - 1 : rows, :] = jnp.zeros((1, LANES), F32)
        own = state[f]
        along[0, f] = jnp.where(lane == 0, 0.0, pltpu.roll(own, 1, 1))
        along[1, f] = jnp.where(lane == LANES - 1, 0.0, pltpu.roll(own, LANES - 1, 1))

    def add_rows(step, carry):
        here = pl.ds(pl.multiple_of(step * step_rows, step_rows), step_rows)
        own = [state[f, here, :] for f in range(12)]
        totals = whirl(own, volume[here, :])
        for number in range(5):
            if number == 0:
                vector = own
            else:
                source = beside if number < 3 else along
                vector = [source[(number - 1) % 2, f, here, :] for f in range(12)]
            totals = product_into(
                totals, lambda e: blocks[number, e, here, :].astype(F32), scales[number, here, :], vector
            )
        for f in range(12):
            out[f, here, :] = totals[f]
        return carry

    lax.fori_loop(0, rows // step_rows, add_rows, 0)
    for number, near, at in ((1, 0, 0), (2, rows - 16, 15)):
        first = (number - 1) * 40
        for e in range(36):
            tile = blocks[number, e, near : near + 16, :].astype(F32)
            edges[first + e : first + e + 1, :] = tile[at : at + 1, :]
        edges[first + 36 : first + 37, :] = scales[number, near + at : near + at + 1, :]
        edges[first + 37 : first + 40, :] = jnp.zeros((3, LANES), F32)


def end_columns_kernel(step_rows, part, blocks, scales, inner, outer, out):
    odd = lax.rem(lax.axis_index("axial"), 2) == 1

    def add_rows(step, carry):
        here = pl.ds(pl.multiple_of(step * step_rows, step_rows), step_rows)
        first, second = inner[here, :], outer[here, :]
        low, high = jnp.where(odd, first, second), jnp.where(odd, second, first)
        lane = iota((step_rows, LANES), 1)
        left_half = lane < LANES // 2
        vector = []
        for f in range(12):
            left = pltpu.roll(low, (LANES - f) % LANES, 1)
            right = pltpu.roll(high, LANES - 1 - 16 - f, 1)
            vector.append(jnp.where(lane == 0, left, jnp.where(lane == LANES - 1, right, 0.0)))
        totals = product_into(
            [part[f, here, :] for f in range(12)],
            lambda e: jnp.where(
                left_half, blocks[3, e, here, :].astype(F32), blocks[4, e, here, :].astype(F32)
            ),
            jnp.where(left_half, scales[3, here, :], scales[4, here, :]),
            vector,
        )
        for f in range(12):
            out[f, here, :] = totals[f]
        return carry

    lax.fori_loop(0, part.shape[1] // step_rows, add_rows, 0)


def pick(table, hot, here):
    found = jnp.dot(table[...], jnp.concatenate([hot, hot], axis=0), preferred_element_type=F32)
    bands = here.shape[0]
    return [
        jnp.sum(jnp.where(here, found[f * bands : (f + 1) * bands, :], 0.0), axis=0, keepdims=True)
        for f in range(table.shape[0] // bands)
    ]


def answer_kernel(width, block, table, arrived, send_hbm, wide, send, sent):
    chunks = wide.shape[0] // 16
    half_rows = table.shape[0] // 13
    copies = []
    for number in range(13, 16):
        wide[pl.ds(number, chunks, stride=16), :] = jnp.zeros((chunks, LANES), F32)
    for base in range(0, chunks, width):
        cell = []
        for g in range(base, base + width):
            at = chunk_base(g, block)
            cell.append(arrived[at : at + 16, :].astype(I32)[12:13, :])
        cell = jnp.concatenate(cell, axis=1)
        row = cell >> 7
        upper = row >= half_rows
        index = (cell & (LANES - 1)) + jnp.where(upper, LANES, 0)
        row = row - jnp.where(upper, half_rows, 0)
        here = iota((half_rows, width * LANES), 0) == row
        value = pick(table, one_hot(index), here)
        for f in range(13):
            for part in range(width):
                at = (base + part) * 16 + f
                wide[at : at + 1, :] = value[f][:, part * LANES : (part + 1) * LANES]
        done = pl.ds(base * 16, width * 16)
        send[done, :] = narrow(wide[done, :])
        copies.append(
            pltpu.make_async_copy(send.at[done, :], send_hbm.at[done, :], sent.at[base // width])
        )
        copies[-1].start()
    for copy in copies:
        copy.wait()


def seal_add_kernel(
    halo_rows, sectors, block, part, arrived, edges, slots, cavity_index,
    link_blocks_hbm, link_scales_hbm,
    *refs,
):
    *halos, out, slot_hot, cell_hot, link_rows, link_scale_rows = refs[:-6]
    left, right, total, link_blocks, link_scales, arrivals = refs[-6:]
    loads = start_loads(
        ((link_blocks_hbm, link_blocks), (link_scales_hbm, link_scales)), arrivals
    )
    chunks = arrived.shape[0] // block * 4
    rows = part.shape[1]
    half_rows = rows // 2
    total[...] = jnp.zeros_like(total)
    deep = left.shape[1] // LANES

    def add_chunks(step, carry):
        for sub in range(deep):
            base = pl.multiple_of(step * (deep // 4 * block) + chunk_base(sub, block), 16)
            tile = arrived[pl.ds(base, 16), :].astype(I32)
            cell = tile[12:13, :]
            tile = tile.astype(F32)
            high, low = halves(tile * jnp.exp2(tile[13:14, :]))
            row = cell >> 7
            column = (cell & (LANES - 1)) + jnp.where(row >= half_rows, LANES, 0)
            row = jnp.where(row >= half_rows, row - half_rows, row)
            cols = slice(sub * LANES, (sub + 1) * LANES)
            right[:, cols] = one_hot(column)
            here = iota((half_rows, LANES), 0) == row
            for f in range(12):
                for number, source in enumerate((high, low)):
                    at = (2 * f + number) * half_rows
                    left[at : at + half_rows, cols] = jnp.where(
                        here, source[f : f + 1, :], 0.0
                    ).astype(BF16)
        total[...] += lax.dot_general(
            left[...], right[...], (((1,), (1,)), ((), ())), preferred_element_type=F32
        )
        return carry

    for c in range(slots.shape[0]):
        cols = slice(c * LANES, (c + 1) * LANES)
        for source, target in ((slots, slot_hot), (cavity_index, cell_hot)):
            target[:, cols] = one_hot(source[c : c + 1, :] & (WIDE - 1))
    lax.fori_loop(0, chunks // deep, add_chunks, 0)
    for f in range(12):
        added = (
            total[2 * f * half_rows : (2 * f + 1) * half_rows, :]
            + total[(2 * f + 1) * half_rows : (2 * f + 2) * half_rows, :]
        )
        out[f, 0:half_rows, :] = part[f, 0:half_rows, :] + added[:, :LANES]
        out[f, half_rows:rows, :] = part[f, half_rows:rows, :] + added[:, LANES:]
    for load in loads:
        load.wait()
    row_count = link_blocks.shape[2] // LANES
    for entry in range(36):
        both = link_blocks[entry].astype(F32)
        for c in range(row_count):
            link_rows[entry * row_count + c : entry * row_count + c + 1, :] = both[
                1:2, c * LANES : (c + 1) * LANES
            ]
    fold_cells(link_scales, link_scale_rows, 2, 0, row_count * LANES)
    me = lax.axis_index("circ")
    for number, step in ((1, sectors - 1), (2, 1)):
        if halo_rows:
            base = pl.multiple_of(lax.rem(me + step, sectors) * block + 64, 16)
            tile = widen(arrived[pl.ds(base, 16), :])
            tile = tile * jnp.exp2(tile[12:13, :])
            vector = [tile[f : f + 1, :] for f in range(12)]
        else:
            vector = [halos[number - 1][f] for f in range(12)]
        at = 0 if number == 1 else rows - 1
        first = (number - 1) * 40
        terms = product_into(
            [None] * 12,
            lambda e: edges[first + e : first + e + 1, :],
            edges[first + 36 : first + 37, :],
            vector,
        )
        for f in range(12):
            out[f, at : at + 1, :] = out[f, at : at + 1, :] + terms[f]


def cavity_kernel(
    state, blocks, scales, links, volume, seal_blocks_hbm, seal_scales_hbm, seal_volume_hbm,
    out, seal_blocks, seal_scales, seal_volume,
    state_rows, block_rows, scale_rows, face_rows, out_rows, arrivals,
):
    loads = start_loads(
        (
            (seal_blocks_hbm, seal_blocks),
            (seal_scales_hbm, seal_scales),
            (seal_volume_hbm, seal_volume),
        ),
        arrivals,
    )
    cells = state.shape[1]
    rows = cells // LANES
    fold_cells(state, state_rows, 12, 0, cells)
    fold_cells(scales, scale_rows, 5, 0, cells)
    fold_cells(links, face_rows, 4, 0, cells)
    for number in range(5):
        for c in range(rows):
            block_rows[pl.ds(number * 36 * rows + c, 36, stride=rows), :] = blocks[
                number, :, c * LANES : (c + 1) * LANES
            ].astype(F32)
    own = [state_rows[f * rows : (f + 1) * rows, :] for f in range(12)]
    totals = whirl(own, volume[...])
    for number in range(5):
        if number == 0:
            vector = own
        else:
            cell = face_rows[(number - 1) * rows : number * rows, :]
            lane, high = cell & (LANES - 1), cell >> 7
            vector = [jnp.zeros((rows, LANES), F32)] * 12
            for r in range(rows):
                here = high == r
                for f in range(12):
                    row = state_rows[f * rows + r : f * rows + r + 1, :]
                    vector[f] = jnp.where(here, lane_take(row, lane), vector[f])
        base = number * 36 * rows
        totals = product_into(
            totals,
            lambda e: block_rows[base + e * rows : base + (e + 1) * rows, :],
            scale_rows[number * rows : (number + 1) * rows, :],
            vector,
        )
    for f in range(12):
        out_rows[f * rows : (f + 1) * rows, :] = totals[f]
    for c in range(rows):
        out[:, c * LANES : (c + 1) * LANES] = out_rows[pl.ds(c, 12, stride=rows), :]
    for load in loads:
        load.wait()


def cavity_add_kernel(
    width, part, arrived, slots, cavity_index, link_rows, scale_rows, slot_hot, cell_hot,
    out, left, table, found, wide,
):
    rows = slots.shape[0]
    chunks = arrived.shape[0] // 16
    groups = chunks // 2
    wide[...] = widen(arrived[...])
    for half in range(2):
        factor = jnp.exp2(wide[pl.ds(half * 16 + 12, groups, stride=32), :])
        for f in range(12):
            high, low = halves(wide[pl.ds(half * 16 + f, groups, stride=32), :] * factor)
            at = pl.ds(f * groups, groups)
            table[at, half * LANES : (half + 1) * LANES] = high.astype(BF16)
            table[at, WIDE + half * LANES : WIDE + (half + 1) * LANES] = low.astype(BF16)
    for base in range(0, rows, width):
        slot = jnp.concatenate([slots[c : c + 1, :] for c in range(base, base + width)], axis=1)
        here = iota((groups, width * LANES), 0) == (slot >> 8)
        value = pick(table, slot_hot[:, base * LANES : (base + width) * LANES], here)
        for f in range(12):
            for number in range(width):
                at = f * rows + base + number
                found[at : at + 1, :] = value[f][:, number * LANES : (number + 1) * LANES]
    vector = [found[f * rows : (f + 1) * rows, :] for f in range(12)]
    terms = product_into(
        [None] * 12,
        lambda e: link_rows[e * rows : (e + 1) * rows, :],
        scale_rows[rows : 2 * rows, :],
        vector,
    )
    parts = [halves(term) for term in terms]
    bands = part.shape[1] // WIDE
    for c in range(rows):
        cell = cavity_index[c : c + 1, :]
        cols = slice(c * LANES, (c + 1) * LANES)
        band = cell >> 8
        zero = jnp.zeros((4, LANES), F32)
        tile = jnp.concatenate(
            [p[0][c : c + 1, :] for p in parts] + [zero] + [p[1][c : c + 1, :] for p in parts] + [zero],
            axis=0,
        )
        for b in range(bands):
            left[b * 32 : (b + 1) * 32, cols] = jnp.where(band == b, tile, 0.0).astype(BF16)
    added = lax.dot_general(
        left[...], cell_hot[...], (((1,), (1,)), ((), ())), preferred_element_type=F32
    )
    for b in range(bands):
        cols = slice(b * WIDE, (b + 1) * WIDE)
        out[:, cols] = part[:, cols] + (added[b * 32 : b * 32 + 12] + added[b * 32 + 16 : b * 32 + 28])


def exchange(values, sectors, chunks):
    if sectors <= chunks:
        shaped = values.reshape(sectors, -1, LANES)
        moved = lax.all_to_all(shaped, "circ", split_axis=0, concat_axis=0, tiled=True)
        return moved.reshape(values.shape)
    each = sectors // chunks
    shaped = values.reshape(chunks, 16, each, LANES // each).transpose(0, 2, 1, 3)
    shaped = shaped.reshape(sectors, 16, LANES // each)
    moved = lax.all_to_all(shaped, "circ", split_axis=0, concat_axis=0, tiled=True)
    moved = moved.reshape(chunks, each, 16, LANES // each).transpose(0, 2, 1, 3)
    return moved.reshape(values.shape)


def on_device(
    seal_state,
    seal_blocks,
    seal_scales,
    seal_volume,
    cavity_state,
    cavity_blocks,
    cavity_scales,
    cavity_links,
    cavity_volume,
    link_owner,
    link_seal,
    link_cavity,
    link_blocks,
    link_scales,
):
    sectors = lax.axis_size("circ")
    segments = lax.axis_size("axial")
    _, seal_rows, _ = seal_state.shape
    cells = cavity_state.shape[1]
    count = link_seal.shape[0]
    rows = count // LANES
    groups = 2 * count // WIDE
    halo_rows = sectors * 2 == groups
    shape = jax.ShapeDtypeStruct
    owner = link_owner.reshape(rows, LANES)
    seal_index = link_seal.reshape(rows, LANES)
    cavity_index = link_cavity.reshape(rows, LANES)
    pair_blocks = link_blocks.transpose(1, 0, 2)

    hbm = lambda a: pltpu.with_memory_space_constraint(a, pltpu.HBM)
    head = (owner, seal_index, cavity_index, cavity_state, pair_blocks, link_scales)
    block = 80 if halo_rows else 64
    preload = (cavity_blocks, cavity_scales, cavity_links, cavity_volume.reshape(-1, LANES))
    send, slots, state, kept_index, *tile = pl.pallas_call(
        functools.partial(interface_kernel, sectors, halo_rows),
        in_specs=[HBM] * 11,
        out_specs=[VMEM] * 9,
        out_shape=[
            shape((groups // 2 * block, LANES), I16),
            shape((rows, LANES), I32),
            shape(seal_state.shape, F32),
        ]
        + [shape(a.shape, a.dtype) for a in head[2:4] + preload],
        scratch_shapes=[
            pltpu.VMEM((72 * rows, LANES), F32),
            pltpu.VMEM((2 * rows, LANES), F32),
            pltpu.VMEM((12 * cells // LANES, LANES), F32),
            pltpu.VMEM((28 * groups, count), BF16),
            pltpu.VMEM((WIDE, count), BF16),
            pltpu.VMEM((groups * 32, LANES), F32),
        ]
        + [pltpu.VMEM(a.shape, a.dtype) for a in head[:2] + head[4:]]
        + [pltpu.SemaphoreType.DMA((11,))],
        compiler_params=PARAMS,
        name="interface",
    )(*[hbm(a) for a in head], hbm(seal_state), *[hbm(a) for a in preload])
    arrived = exchange(send, sectors, 2 * groups)

    faces, table = pl.pallas_call(
        face_kernel,
        in_specs=[VMEM],
        out_specs=[VMEM] * 2,
        out_shape=[
            shape((seal_rows, LANES), F32),
            shape((13 * seal_rows // 2, 2 * WIDE), BF16),
        ],
        compiler_params=PARAMS,
        name="faces",
    )(state)
    swaps = lambda begin: [
        pair for i in range(begin, segments - 1, 2) for pair in ((i, i + 1), (i + 1, i))
    ]
    inner = lax.ppermute(faces, "axial", swaps(0))
    outer = lax.ppermute(faces, "axial", swaps(1))
    if halo_rows:
        halos = ()
    else:
        first, last = seal_state[:, :1], seal_state[:, -1:]
        halos = (
            lax.ppermute(last, "circ", [(i, (i + 1) % sectors) for i in range(sectors)]),
            lax.ppermute(first, "circ", [((i + 1) % sectors, i) for i in range(sectors)]),
        )

    kept = (seal_blocks, seal_scales, seal_volume)
    cavity_part, kept_blocks, kept_scales, kept_volume = pl.pallas_call(
        cavity_kernel,
        in_specs=[VMEM] * 5 + [HBM] * 3,
        out_specs=[VMEM] * 4,
        out_shape=[shape((12, cells), F32)] + [shape(a.shape, a.dtype) for a in kept],
        scratch_shapes=[
            pltpu.VMEM((12 * cells // LANES, LANES), F32),
            pltpu.VMEM((180 * cells // LANES, LANES), F32),
            pltpu.VMEM((5 * cells // LANES, LANES), F32),
            pltpu.VMEM((4 * cells // LANES, LANES), I32),
            pltpu.VMEM((12 * cells // LANES, LANES), F32),
            pltpu.SemaphoreType.DMA((3,)),
        ],
        compiler_params=PARAMS,
        cost_estimate=pl.CostEstimate(flops=10**6, bytes_accessed=10**7, transcendentals=0),
        name="cavity",
    )(*tile, *[hbm(a) for a in kept])

    seal_part, edges = pl.pallas_call(
        functools.partial(seal_kernel, 16),
        in_specs=[VMEM] * 4,
        out_specs=[VMEM] * 2,
        out_shape=[shape(seal_state.shape, F32), shape((80, LANES), F32)],
        scratch_shapes=[
            pltpu.VMEM((2,) + seal_state.shape, F32),
            pltpu.VMEM((2,) + seal_state.shape, F32),
        ],
        compiler_params=PARAMS,
        cost_estimate=pl.CostEstimate(flops=10**6, bytes_accessed=10**7, transcendentals=0),
        name="seal",
    )(state, kept_blocks, kept_scales, kept_volume)
    seal_part = pl.pallas_call(
        functools.partial(end_columns_kernel, 16),
        in_specs=[VMEM] * 5,
        out_specs=VMEM,
        out_shape=shape(seal_state.shape, F32),
        compiler_params=PARAMS,
        name="end_columns",
    )(seal_part, kept_blocks, kept_scales, inner, outer)

    arrived, seal_part, cavity_part = lax.optimization_barrier((arrived, seal_part, cavity_part))
    width = 8
    answers = pl.pallas_call(
        functools.partial(answer_kernel, width, block),
        in_specs=[VMEM] * 2,
        out_specs=HBM,
        out_shape=pltpu.HBM((groups * 32, LANES), I16),
        scratch_shapes=[
            pltpu.VMEM((groups * 32, LANES), F32),
            pltpu.VMEM((groups * 32, LANES), I16),
            pltpu.SemaphoreType.DMA((2 * groups // width,)),
        ],
        compiler_params=PARAMS,
        name="answers",
    )(table, arrived)
    returned = exchange(answers, sectors, 2 * groups)

    deep = 8
    seal_result, slot_hot, cell_hot, link_rows, link_scale_rows = pl.pallas_call(
        functools.partial(seal_add_kernel, halo_rows, sectors, block),
        in_specs=[VMEM] * 5 + [HBM] * 2 + [VMEM] * len(halos),
        out_specs=[VMEM] * 5,
        out_shape=[shape(seal_state.shape, F32)]
        + [shape((WIDE, count), BF16)] * 2
        + [shape((36 * rows, LANES), F32), shape((2 * rows, LANES), F32)],
        scratch_shapes=[
            pltpu.VMEM((12 * seal_rows, deep * LANES), BF16),
            pltpu.VMEM((WIDE, deep * LANES), BF16),
            pltpu.VMEM((12 * seal_rows, WIDE), F32),
            pltpu.VMEM(pair_blocks.shape, BF16),
            pltpu.VMEM(link_scales.shape, F32),
            pltpu.SemaphoreType.DMA((2,)),
        ],
        compiler_params=PARAMS,
        cost_estimate=pl.CostEstimate(flops=10**6, bytes_accessed=10**7, transcendentals=0),
        name="seal_add",
    )(seal_part, arrived, edges, slots, kept_index, hbm(pair_blocks), hbm(link_scales), *halos)

    cavity_result = pl.pallas_call(
        functools.partial(cavity_add_kernel, 8),
        in_specs=[VMEM] * 8,
        out_specs=VMEM,
        out_shape=shape((12, cells), F32),
        scratch_shapes=[
            pltpu.VMEM((32 * cells // WIDE, count), BF16),
            pltpu.VMEM((12 * groups, 2 * WIDE), BF16),
            pltpu.VMEM((12 * rows, LANES), F32),
            pltpu.VMEM((groups * 32, LANES), F32),
        ],
        compiler_params=PARAMS,
        name="cavity_add",
    )(cavity_part, returned, slots, kept_index, link_rows, link_scale_rows, slot_hot, cell_hot)
    return seal_result, cavity_result


def solution(mesh):
    return jax.shard_map(
        on_device,
        mesh=mesh,
        in_specs=(
            P(None, "circ", "axial"),
            P(None, None, "circ", "axial"),
            P(None, "circ", "axial"),
            P("circ", "axial"),
            P(None, ("circ", "axial")),
            P(None, None, ("circ", "axial")),
            P(None, ("circ", "axial")),
            P(None, ("circ", "axial")),
            P(("circ", "axial")),
            P(("circ", "axial"), None),
            P(("circ", "axial")),
            P(("circ", "axial")),
            P(None, None, ("circ", "axial")),
            P(None, ("circ", "axial")),
        ),
        out_specs=(P(None, "circ", "axial"), P(None, ("circ", "axial"))),
        check_vma=False,
    )
```

```python
import functools
import jax
import jax.numpy as jnp
from jax import lax
from jax.experimental import pallas as pl
from jax.experimental.pallas import tpu as pltpu
from jax.sharding import PartitionSpec as P

whirl_rate = 0.6
F32, BF16, I32, I16 = jnp.float32, jnp.bfloat16, jnp.int32, jnp.int16
LANES = 128
WIDE = 256
PARAMS = pltpu.CompilerParams(vmem_limit_bytes=16 * 1024 * 1024)
VMEM = pl.BlockSpec(memory_space=pltpu.VMEM)
HBM = pl.BlockSpec(memory_space=pltpu.HBM)


def iota(shape, axis):
    return lax.broadcasted_iota(I32, shape, axis)


def lane_take(row, index):
    table = jnp.broadcast_to(row, index.shape)
    return jnp.take_along_axis(table, index, axis=1, mode="promise_in_bounds")


def one_hot(index):
    return jnp.where(iota((WIDE, index.shape[1]), 0) == index, 1.0, 0.0).astype(BF16)


def halves(value):
    high = value.astype(BF16).astype(F32)
    return high, value - high


def coded(values):
    top = functools.reduce(jnp.maximum, [jnp.abs(v) for v in values])
    power = jnp.ceil(jnp.log2(jnp.maximum(top, 2.0**-100) * (1.0 / 32000.0)))
    factor = jnp.exp2(-power)
    return [jnp.round(v * factor) for v in values], power


def integer_halves(value):
    high = 256.0 * jnp.floor(value * (1.0 / 256.0))
    return high, value - high


def narrow(value):
    return value.astype(I32).astype(I16)


def widen(value):
    return value.astype(I32).astype(F32)


def chunk_base(chunk, block):
    return (chunk // 4) * block + (chunk % 4) * 16


def product_into(totals, entry, factor, vector):
    for row in range(6):
        real_part = imag_part = None
        for col in range(6):
            element = entry(6 * row + col)
            real_term, imag_term = element * vector[col], element * vector[6 + col]
            real_part = real_term if real_part is None else real_part + real_term
            imag_part = imag_term if imag_part is None else imag_part + imag_term
        real_part, imag_part = factor * real_part, factor * imag_part
        totals[row] = real_part if totals[row] is None else totals[row] + real_part
        totals[6 + row] = imag_part if totals[6 + row] is None else totals[6 + row] + imag_part
    return totals


def whirl(vector, volume):
    weight = whirl_rate * volume
    return [-weight * v for v in vector[6:]] + [weight * v for v in vector[:6]]


def fold_cells(source, target, count, base, cells):
    rows = cells // LANES
    for chunk in range(rows):
        target[pl.ds(base + chunk, count, stride=rows), :] = source[:, chunk * LANES : (chunk + 1) * LANES]


def interface_kernel(
    sectors, halo_rows, owner_hbm, seal_index_hbm, cavity_index_hbm, state_hbm, blocks_hbm,
    scales_hbm, seal_hbm, tile_blocks_hbm, tile_scales_hbm, tile_links_hbm, tile_volume_hbm,
    send, slots, seal, cavity_index, state, tile_blocks, tile_scales, tile_links, tile_volume,
    block_rows, scale_rows, state_rows, left, right, wide, owner, seal_index, blocks, scales,
    arrivals,
):
    loads = start_loads(
        (
            (owner_hbm, owner),
            (blocks_hbm, blocks),
            (scales_hbm, scales),
            (state_hbm, state),
            (cavity_index_hbm, cavity_index),
            (seal_index_hbm, seal_index),
            (seal_hbm, seal),
            (tile_blocks_hbm, tile_blocks),
            (tile_scales_hbm, tile_scales),
            (tile_links_hbm, tile_links),
            (tile_volume_hbm, tile_volume),
        ),
        arrivals,
    )
    loads[0].wait()
    rows = owner.shape[0]
    capacity = 2 * rows * LANES // sectors
    sector_id = iota((sectors, LANES), 0)
    hot = [
        jnp.where(sector_id == owner[c : c + 1, :], 1.0, 0.0).astype(F32) for c in range(rows)
    ]
    stacked = jnp.concatenate(hot, axis=0).astype(BF16)
    before = (iota((LANES, LANES), 0) < iota((LANES, LANES), 1)).astype(F32).astype(BF16)
    prefix = jnp.dot(stacked, before, preferred_element_type=F32)
    totals = jnp.dot(stacked, jnp.ones((LANES, LANES), BF16), preferred_element_type=F32)
    offset = jnp.zeros((sectors, LANES), F32)
    for c in range(rows):
        part = slice(c * sectors, (c + 1) * sectors)
        place = jnp.sum(hot[c] * (prefix[part] + offset), axis=0, keepdims=True)
        slots[c : c + 1, :] = owner[c : c + 1, :] * capacity + place.astype(I32)
        offset = offset + totals[part]
    for load in loads[1:6]:
        load.wait()
    for entry in range(36):
        both = blocks[entry].astype(F32)
        for c in range(rows):
            block_rows[entry * rows + c : entry * rows + c + 1, :] = both[
                0:1, c * LANES : (c + 1) * LANES
            ]
    fold_cells(scales, scale_rows, 2, 0, rows * LANES)
    fold_cells(state, state_rows, 12, 0, state.shape[1])
    tile_rows = state.shape[1] // LANES
    cell = cavity_index[...]
    lane, high = cell & (LANES - 1), cell >> 7
    vector = [jnp.zeros((rows, LANES), F32)] * 12
    for r in range(tile_rows):
        here = high == r
        for f in range(12):
            row = state_rows[f * tile_rows + r : f * tile_rows + r + 1, :]
            vector[f] = jnp.where(here, lane_take(row, lane), vector[f])
    terms = product_into(
        [None] * 12, lambda e: block_rows[e * rows : (e + 1) * rows, :], scale_rows[0:rows, :], vector
    )
    terms, power = coded(terms)
    terms = terms + [seal_index[...].astype(F32), power]
    parts = [half for term in terms for half in integer_halves(term)]
    groups = 2 * rows * LANES // WIDE
    for c in range(rows):
        slot = slots[c : c + 1, :]
        cols = slice(c * LANES, (c + 1) * LANES)
        right[:, cols] = one_hot(slot & (WIDE - 1))
        here = iota((groups, LANES), 0) == (slot >> 8)
        for number, part in enumerate(parts):
            left[number * groups : (number + 1) * groups, cols] = jnp.where(
                here, part[c : c + 1, :], 0.0
            ).astype(BF16)
    moved = lax.dot_general(
        left[...], right[...], (((1,), (1,)), ((), ())), preferred_element_type=F32
    )
    for number in range(14):
        pair = moved[2 * number * groups : (2 * number + 2) * groups]
        value = pair[:groups] + pair[groups:]
        for half in range(2):
            wide[pl.ds(half * 16 + number, groups, stride=32), :] = value[
                :, half * LANES : (half + 1) * LANES
            ]
    for number in range(14, 16):
        wide[pl.ds(number, 2 * groups, stride=16), :] = jnp.zeros((2 * groups, LANES), F32)
    for load in loads[6:]:
        load.wait()
    block = send.shape[0] * 2 // groups
    for at in range(0, groups // 2):
        send[at * block : at * block + 64, :] = narrow(wide[at * 64 : at * 64 + 64, :])
    if halo_rows:
        me = lax.axis_index("circ")
        zero = jnp.zeros((16, LANES), I16)
        for at in range(0, groups // 2):
            send[at * block + 64 : at * block + 80, :] = zero
        for step, row in ((1, seal.shape[1] - 1), (sectors - 1, 0)):
            base = pl.multiple_of(lax.rem(me + step, sectors) * block + 64, 16)
            values, power = coded([seal[f, row : row + 1, :] for f in range(12)])
            tile = jnp.concatenate(values + [power] + [jnp.zeros((3, LANES), F32)], axis=0)
            send[pl.ds(base, 16), :] = narrow(tile)


def start_loads(pairs, arrivals):
    loads = [
        pltpu.make_async_copy(source, target, arrivals.at[number])
        for number, (source, target) in enumerate(pairs)
    ]
    for load in loads:
        load.start()
    return loads


def face_kernel(state, faces, table):
    lane = iota(faces.shape, 1)
    half_rows = faces.shape[0] // 2
    total = jnp.zeros(faces.shape, F32)
    for f in range(12):
        total = jnp.where(lane == f, pltpu.roll(state[f], f + 1, 1), total)
        total = jnp.where(lane == 16 + f, pltpu.roll(state[f], 16 + f, 1), total)
    faces[...] = total
    for half in range(2):
        here = slice(half * half_rows, (half + 1) * half_rows)
        values, power = coded([state[f, here, :] for f in range(12)])
        for f, value in enumerate(values + [power]):
            high, low = integer_halves(value)
            at = pl.ds(f * half_rows, half_rows)
            table[at, half * LANES : (half + 1) * LANES] = high.astype(BF16)
            table[at, WIDE + half * LANES : WIDE + (half + 1) * LANES] = low.astype(BF16)


def seal_kernel(step_rows, state, blocks, scales, volume, out, edges, beside, along):
    rows = state.shape[1]
    lane = iota((rows, LANES), 1)
    for f in range(12):
        beside[0, f, 1:rows, :] = state[f, 0 : rows - 1, :]
        beside[0, f, 0:1, :] = jnp.zeros((1, LANES), F32)
        beside[1, f, 0 : rows - 1, :] = state[f, 1:rows, :]
        beside[1, f, rows - 1 : rows, :] = jnp.zeros((1, LANES), F32)
        own = state[f]
        along[0, f] = jnp.where(lane == 0, 0.0, pltpu.roll(own, 1, 1))
        along[1, f] = jnp.where(lane == LANES - 1, 0.0, pltpu.roll(own, LANES - 1, 1))

    def add_rows(step, carry):
        here = pl.ds(pl.multiple_of(step * step_rows, step_rows), step_rows)
        own = [state[f, here, :] for f in range(12)]
        totals = whirl(own, volume[here, :])
        for number in range(5):
            if number == 0:
                vector = own
            else:
                source = beside if number < 3 else along
                vector = [source[(number - 1) % 2, f, here, :] for f in range(12)]
            totals = product_into(
                totals, lambda e: blocks[number, e, here, :].astype(F32), scales[number, here, :], vector
            )
        for f in range(12):
            out[f, here, :] = totals[f]
        return carry

    lax.fori_loop(0, rows // step_rows, add_rows, 0)
    for number, near, at in ((1, 0, 0), (2, rows - 16, 15)):
        first = (number - 1) * 40
        for e in range(36):
            tile = blocks[number, e, near : near + 16, :].astype(F32)
            edges[first + e : first + e + 1, :] = tile[at : at + 1, :]
        edges[first + 36 : first + 37, :] = scales[number, near + at : near + at + 1, :]
        edges[first + 37 : first + 40, :] = jnp.zeros((3, LANES), F32)


def end_columns_kernel(step_rows, part, blocks, scales, inner, outer, out):
    odd = lax.rem(lax.axis_index("axial"), 2) == 1

    def add_rows(step, carry):
        here = pl.ds(pl.multiple_of(step * step_rows, step_rows), step_rows)
        first, second = inner[here, :], outer[here, :]
        low, high = jnp.where(odd, first, second), jnp.where(odd, second, first)
        lane = iota((step_rows, LANES), 1)
        left_half = lane < LANES // 2
        vector = []
        for f in range(12):
            left = pltpu.roll(low, (LANES - f) % LANES, 1)
            right = pltpu.roll(high, LANES - 1 - 16 - f, 1)
            vector.append(jnp.where(lane == 0, left, jnp.where(lane == LANES - 1, right, 0.0)))
        totals = product_into(
            [part[f, here, :] for f in range(12)],
            lambda e: jnp.where(
                left_half, blocks[3, e, here, :].astype(F32), blocks[4, e, here, :].astype(F32)
            ),
            jnp.where(left_half, scales[3, here, :], scales[4, here, :]),
            vector,
        )
        for f in range(12):
            out[f, here, :] = totals[f]
        return carry

    lax.fori_loop(0, part.shape[1] // step_rows, add_rows, 0)


def pick(table, hot, here):
    found = jnp.dot(table[...], jnp.concatenate([hot, hot], axis=0), preferred_element_type=F32)
    bands = here.shape[0]
    return [
        jnp.sum(jnp.where(here, found[f * bands : (f + 1) * bands, :], 0.0), axis=0, keepdims=True)
        for f in range(table.shape[0] // bands)
    ]


def answer_kernel(width, block, table, arrived, send_hbm, wide, send, sent):
    chunks = wide.shape[0] // 16
    half_rows = table.shape[0] // 13
    copies = []
    for number in range(13, 16):
        wide[pl.ds(number, chunks, stride=16), :] = jnp.zeros((chunks, LANES), F32)
    for base in range(0, chunks, width):
        cell = []
        for g in range(base, base + width):
            at = chunk_base(g, block)
            cell.append(arrived[at : at + 16, :].astype(I32)[12:13, :])
        cell = jnp.concatenate(cell, axis=1)
        row = cell >> 7
        upper = row >= half_rows
        index = (cell & (LANES - 1)) + jnp.where(upper, LANES, 0)
        row = row - jnp.where(upper, half_rows, 0)
        here = iota((half_rows, width * LANES), 0) == row
        value = pick(table, one_hot(index), here)
        for f in range(13):
            for part in range(width):
                at = (base + part) * 16 + f
                wide[at : at + 1, :] = value[f][:, part * LANES : (part + 1) * LANES]
        done = pl.ds(base * 16, width * 16)
        send[done, :] = narrow(wide[done, :])
        copies.append(
            pltpu.make_async_copy(send.at[done, :], send_hbm.at[done, :], sent.at[base // width])
        )
        copies[-1].start()
    for copy in copies:
        copy.wait()


def seal_add_kernel(
    halo_rows, sectors, block, part, arrived, edges, slots, cavity_index,
    link_blocks_hbm, link_scales_hbm,
    *refs,
):
    *halos, out, slot_hot, cell_hot, link_rows, link_scale_rows = refs[:-6]
    left, right, total, link_blocks, link_scales, arrivals = refs[-6:]
    loads = start_loads(
        ((link_blocks_hbm, link_blocks), (link_scales_hbm, link_scales)), arrivals
    )
    chunks = arrived.shape[0] // block * 4
    rows = part.shape[1]
    half_rows = rows // 2
    total[...] = jnp.zeros_like(total)
    deep = left.shape[1] // LANES

    def add_chunks(step, carry):
        for sub in range(deep):
            base = pl.multiple_of(step * (deep // 4 * block) + chunk_base(sub, block), 16)
            tile = arrived[pl.ds(base, 16), :].astype(I32)
            cell = tile[12:13, :]
            tile = tile.astype(F32)
            high, low = halves(tile * jnp.exp2(tile[13:14, :]))
            row = cell >> 7
            column = (cell & (LANES - 1)) + jnp.where(row >= half_rows, LANES, 0)
            row = jnp.where(row >= half_rows, row - half_rows, row)
            cols = slice(sub * LANES, (sub + 1) * LANES)
            right[:, cols] = one_hot(column)
            here = iota((half_rows, LANES), 0) == row
            for f in range(12):
                for number, source in enumerate((high, low)):
                    at = (2 * f + number) * half_rows
                    left[at : at + half_rows, cols] = jnp.where(
                        here, source[f : f + 1, :], 0.0
                    ).astype(BF16)
        total[...] += lax.dot_general(
            left[...], right[...], (((1,), (1,)), ((), ())), preferred_element_type=F32
        )
        return carry

    for c in range(slots.shape[0]):
        cols = slice(c * LANES, (c + 1) * LANES)
        for source, target in ((slots, slot_hot), (cavity_index, cell_hot)):
            target[:, cols] = one_hot(source[c : c + 1, :] & (WIDE - 1))
    lax.fori_loop(0, chunks // deep, add_chunks, 0)
    for f in range(12):
        added = (
            total[2 * f * half_rows : (2 * f + 1) * half_rows, :]
            + total[(2 * f + 1) * half_rows : (2 * f + 2) * half_rows, :]
        )
        out[f, 0:half_rows, :] = part[f, 0:half_rows, :] + added[:, :LANES]
        out[f, half_rows:rows, :] = part[f, half_rows:rows, :] + added[:, LANES:]
    for load in loads:
        load.wait()
    row_count = link_blocks.shape[2] // LANES
    for entry in range(36):
        both = link_blocks[entry].astype(F32)
        for c in range(row_count):
            link_rows[entry * row_count + c : entry * row_count + c + 1, :] = both[
                1:2, c * LANES : (c + 1) * LANES
            ]
    fold_cells(link_scales, link_scale_rows, 2, 0, row_count * LANES)
    me = lax.axis_index("circ")
    for number, step in ((1, sectors - 1), (2, 1)):
        if halo_rows:
            base = pl.multiple_of(lax.rem(me + step, sectors) * block + 64, 16)
            tile = widen(arrived[pl.ds(base, 16), :])
            tile = tile * jnp.exp2(tile[12:13, :])
            vector = [tile[f : f + 1, :] for f in range(12)]
        else:
            vector = [halos[number - 1][f] for f in range(12)]
        at = 0 if number == 1 else rows - 1
        first = (number - 1) * 40
        terms = product_into(
            [None] * 12,
            lambda e: edges[first + e : first + e + 1, :],
            edges[first + 36 : first + 37, :],
            vector,
        )
        for f in range(12):
            out[f, at : at + 1, :] = out[f, at : at + 1, :] + terms[f]


def cavity_kernel(
    state, blocks, scales, links, volume, seal_blocks_hbm, seal_scales_hbm, seal_volume_hbm,
    out, seal_blocks, seal_scales, seal_volume,
    state_rows, block_rows, scale_rows, face_rows, out_rows, arrivals,
):
    loads = start_loads(
        (
            (seal_blocks_hbm, seal_blocks),
            (seal_scales_hbm, seal_scales),
            (seal_volume_hbm, seal_volume),
        ),
        arrivals,
    )
    cells = state.shape[1]
    rows = cells // LANES
    fold_cells(state, state_rows, 12, 0, cells)
    fold_cells(scales, scale_rows, 5, 0, cells)
    fold_cells(links, face_rows, 4, 0, cells)
    for number in range(5):
        for c in range(rows):
            block_rows[pl.ds(number * 36 * rows + c, 36, stride=rows), :] = blocks[
                number, :, c * LANES : (c + 1) * LANES
            ].astype(F32)
    own = [state_rows[f * rows : (f + 1) * rows, :] for f in range(12)]
    totals = whirl(own, volume[...])
    for number in range(5):
        if number == 0:
            vector = own
        else:
            cell = face_rows[(number - 1) * rows : number * rows, :]
            lane, high = cell & (LANES - 1), cell >> 7
            vector = [jnp.zeros((rows, LANES), F32)] * 12
            for r in range(rows):
                here = high == r
                for f in range(12):
                    row = state_rows[f * rows + r : f * rows + r + 1, :]
                    vector[f] = jnp.where(here, lane_take(row, lane), vector[f])
        base = number * 36 * rows
        totals = product_into(
            totals,
            lambda e: block_rows[base + e * rows : base + (e + 1) * rows, :],
            scale_rows[number * rows : (number + 1) * rows, :],
            vector,
        )
    for f in range(12):
        out_rows[f * rows : (f + 1) * rows, :] = totals[f]
    for c in range(rows):
        out[:, c * LANES : (c + 1) * LANES] = out_rows[pl.ds(c, 12, stride=rows), :]
    for load in loads:
        load.wait()


def cavity_add_kernel(
    width, part, arrived, slots, cavity_index, link_rows, scale_rows, slot_hot, cell_hot,
    out, left, table, found, wide,
):
    rows = slots.shape[0]
    chunks = arrived.shape[0] // 16
    groups = chunks // 2
    wide[...] = widen(arrived[...])
    for half in range(2):
        factor = jnp.exp2(wide[pl.ds(half * 16 + 12, groups, stride=32), :])
        for f in range(12):
            high, low = halves(wide[pl.ds(half * 16 + f, groups, stride=32), :] * factor)
            at = pl.ds(f * groups, groups)
            table[at, half * LANES : (half + 1) * LANES] = high.astype(BF16)
            table[at, WIDE + half * LANES : WIDE + (half + 1) * LANES] = low.astype(BF16)
    for base in range(0, rows, width):
        slot = jnp.concatenate([slots[c : c + 1, :] for c in range(base, base + width)], axis=1)
        here = iota((groups, width * LANES), 0) == (slot >> 8)
        value = pick(table, slot_hot[:, base * LANES : (base + width) * LANES], here)
        for f in range(12):
            for number in range(width):
                at = f * rows + base + number
                found[at : at + 1, :] = value[f][:, number * LANES : (number + 1) * LANES]
    vector = [found[f * rows : (f + 1) * rows, :] for f in range(12)]
    terms = product_into(
        [None] * 12,
        lambda e: link_rows[e * rows : (e + 1) * rows, :],
        scale_rows[rows : 2 * rows, :],
        vector,
    )
    parts = [halves(term) for term in terms]
    bands = part.shape[1] // WIDE
    for c in range(rows):
        cell = cavity_index[c : c + 1, :]
        cols = slice(c * LANES, (c + 1) * LANES)
        band = cell >> 8
        zero = jnp.zeros((4, LANES), F32)
        tile = jnp.concatenate(
            [p[0][c : c + 1, :] for p in parts] + [zero] + [p[1][c : c + 1, :] for p in parts] + [zero],
            axis=0,
        )
        for b in range(bands):
            left[b * 32 : (b + 1) * 32, cols] = jnp.where(band == b, tile, 0.0).astype(BF16)
    added = lax.dot_general(
        left[...], cell_hot[...], (((1,), (1,)), ((), ())), preferred_element_type=F32
    )
    for b in range(bands):
        cols = slice(b * WIDE, (b + 1) * WIDE)
        out[:, cols] = part[:, cols] + (added[b * 32 : b * 32 + 12] + added[b * 32 + 16 : b * 32 + 28])


def exchange(values, sectors, chunks):
    if sectors <= chunks:
        shaped = values.reshape(sectors, -1, LANES)
        moved = lax.all_to_all(shaped, "circ", split_axis=0, concat_axis=0, tiled=True)
        return moved.reshape(values.shape)
    each = sectors // chunks
    shaped = values.reshape(chunks, 16, each, LANES // each).transpose(0, 2, 1, 3)
    shaped = shaped.reshape(sectors, 16, LANES // each)
    moved = lax.all_to_all(shaped, "circ", split_axis=0, concat_axis=0, tiled=True)
    moved = moved.reshape(chunks, each, 16, LANES // each).transpose(0, 2, 1, 3)
    return moved.reshape(values.shape)


def on_device(
    seal_state,
    seal_blocks,
    seal_scales,
    seal_volume,
    cavity_state,
    cavity_blocks,
    cavity_scales,
    cavity_links,
    cavity_volume,
    link_owner,
    link_seal,
    link_cavity,
    link_blocks,
    link_scales,
):
    sectors = lax.axis_size("circ")
    segments = lax.axis_size("axial")
    _, seal_rows, _ = seal_state.shape
    cells = cavity_state.shape[1]
    count = link_seal.shape[0]
    rows = count // LANES
    groups = 2 * count // WIDE
    halo_rows = sectors * 2 == groups
    shape = jax.ShapeDtypeStruct
    owner = link_owner.reshape(rows, LANES)
    seal_index = link_seal.reshape(rows, LANES)
    cavity_index = link_cavity.reshape(rows, LANES)
    pair_blocks = link_blocks.transpose(1, 0, 2)

    hbm = lambda a: pltpu.with_memory_space_constraint(a, pltpu.HBM)
    head = (owner, seal_index, cavity_index, cavity_state, pair_blocks, link_scales)
    block = 80 if halo_rows else 64
    preload = (cavity_blocks, cavity_scales, cavity_links, cavity_volume.reshape(-1, LANES))
    send, slots, state, kept_index, *tile = pl.pallas_call(
        functools.partial(interface_kernel, sectors, halo_rows),
        in_specs=[HBM] * 11,
        out_specs=[VMEM] * 9,
        out_shape=[
            shape((groups // 2 * block, LANES), I16),
            shape((rows, LANES), I32),
            shape(seal_state.shape, F32),
        ]
        + [shape(a.shape, a.dtype) for a in head[2:4] + preload],
        scratch_shapes=[
            pltpu.VMEM((36 * rows, LANES), F32),
            pltpu.VMEM((8 * rows, LANES), F32),
            pltpu.VMEM((16 * cells // LANES, LANES), F32),
            pltpu.VMEM((28 * groups, count), BF16),
            pltpu.VMEM((WIDE, count), BF16),
            pltpu.VMEM((groups * 32, LANES), F32),
        ]
        + [pltpu.VMEM(a.shape, a.dtype) for a in head[:2] + head[4:]]
        + [pltpu.SemaphoreType.DMA((11,))],
        compiler_params=PARAMS,
        name="interface",
    )(*[hbm(a) for a in head], hbm(seal_state), *[hbm(a) for a in preload])
    arrived = exchange(send, sectors, 2 * groups)

    faces, table = pl.pallas_call(
        face_kernel,
        in_specs=[VMEM],
        out_specs=[VMEM] * 2,
        out_shape=[
            shape((seal_rows, LANES), F32),
            shape((13 * seal_rows // 2, 2 * WIDE), BF16),
        ],
        compiler_params=PARAMS,
        name="faces",
    )(state)
    swaps = lambda begin: [
        pair for i in range(begin, segments - 1, 2) for pair in ((i, i + 1), (i + 1, i))
    ]
    inner = lax.ppermute(faces, "axial", swaps(0))
    outer = lax.ppermute(faces, "axial", swaps(1))
    if halo_rows:
        halos = ()
    else:
        first, last = seal_state[:, :1], seal_state[:, -1:]
        halos = (
            lax.ppermute(last, "circ", [(i, (i + 1) % sectors) for i in range(sectors)]),
            lax.ppermute(first, "circ", [((i + 1) % sectors, i) for i in range(sectors)]),
        )

    kept = (seal_blocks, seal_scales, seal_volume)
    cavity_part, kept_blocks, kept_scales, kept_volume = pl.pallas_call(
        cavity_kernel,
        in_specs=[VMEM] * 5 + [HBM] * 3,
        out_specs=[VMEM] * 4,
        out_shape=[shape((12, cells), F32)] + [shape(a.shape, a.dtype) for a in kept],
        scratch_shapes=[
            pltpu.VMEM((16 * cells // LANES, LANES), F32),
            pltpu.VMEM((184 * cells // LANES, LANES), F32),
            pltpu.VMEM((8 * cells // LANES, LANES), F32),
            pltpu.VMEM((8 * cells // LANES, LANES), I32),
            pltpu.VMEM((16 * cells // LANES, LANES), F32),
            pltpu.SemaphoreType.DMA((3,)),
        ],
        compiler_params=PARAMS,
        cost_estimate=pl.CostEstimate(flops=10**6, bytes_accessed=10**7, transcendentals=0),
        name="cavity",
    )(*tile, *[hbm(a) for a in kept])

    seal_part, edges = pl.pallas_call(
        functools.partial(seal_kernel, 16),
        in_specs=[VMEM] * 4,
        out_specs=[VMEM] * 2,
        out_shape=[shape(seal_state.shape, F32), shape((80, LANES), F32)],
        scratch_shapes=[
            pltpu.VMEM((2,) + seal_state.shape, F32),
            pltpu.VMEM((2,) + seal_state.shape, F32),
        ],
        compiler_params=PARAMS,
        cost_estimate=pl.CostEstimate(flops=10**6, bytes_accessed=10**7, transcendentals=0),
        name="seal",
    )(state, kept_blocks, kept_scales, kept_volume)
    seal_part = pl.pallas_call(
        functools.partial(end_columns_kernel, 16),
        in_specs=[VMEM] * 5,
        out_specs=VMEM,
        out_shape=shape(seal_state.shape, F32),
        compiler_params=PARAMS,
        name="end_columns",
    )(seal_part, kept_blocks, kept_scales, inner, outer)

    arrived, seal_part, cavity_part = lax.optimization_barrier((arrived, seal_part, cavity_part))
    width = 8
    answers = pl.pallas_call(
        functools.partial(answer_kernel, width, block),
        in_specs=[VMEM] * 2,
        out_specs=HBM,
        out_shape=pltpu.HBM((groups * 32, LANES), I16),
        scratch_shapes=[
            pltpu.VMEM((groups * 32, LANES), F32),
            pltpu.VMEM((groups * 32, LANES), I16),
            pltpu.SemaphoreType.DMA((2 * groups // width,)),
        ],
        compiler_params=PARAMS,
        name="answers",
    )(table, arrived)
    returned = exchange(answers, sectors, 2 * groups)

    deep = 8
    seal_result, slot_hot, cell_hot, link_rows, link_scale_rows = pl.pallas_call(
        functools.partial(seal_add_kernel, halo_rows, sectors, block),
        in_specs=[VMEM] * 5 + [HBM] * 2 + [VMEM] * len(halos),
        out_specs=[VMEM] * 5,
        out_shape=[shape(seal_state.shape, F32)]
        + [shape((WIDE, count), BF16)] * 2
        + [shape((36 * rows, LANES), F32), shape((8 * rows, LANES), F32)],
        scratch_shapes=[
            pltpu.VMEM((12 * seal_rows, deep * LANES), BF16),
            pltpu.VMEM((WIDE, deep * LANES), BF16),
            pltpu.VMEM((12 * seal_rows, WIDE), F32),
            pltpu.VMEM(pair_blocks.shape, BF16),
            pltpu.VMEM(link_scales.shape, F32),
            pltpu.SemaphoreType.DMA((2,)),
        ],
        compiler_params=PARAMS,
        cost_estimate=pl.CostEstimate(flops=10**6, bytes_accessed=10**7, transcendentals=0),
        name="seal_add",
    )(seal_part, arrived, edges, slots, kept_index, hbm(pair_blocks), hbm(link_scales), *halos)

    cavity_result = pl.pallas_call(
        functools.partial(cavity_add_kernel, 8),
        in_specs=[VMEM] * 8,
        out_specs=VMEM,
        out_shape=shape((12, cells), F32),
        scratch_shapes=[
            pltpu.VMEM((32 * cells // WIDE, count), BF16),
            pltpu.VMEM((12 * groups, 2 * WIDE), BF16),
            pltpu.VMEM((12 * rows, LANES), F32),
            pltpu.VMEM((groups * 32, LANES), F32),
        ],
        compiler_params=PARAMS,
        name="cavity_add",
    )(cavity_part, returned, slots, kept_index, link_rows, link_scale_rows, slot_hot, cell_hot)
    return seal_result, cavity_result


def solution(mesh):
    return jax.shard_map(
        on_device,
        mesh=mesh,
        in_specs=(
            P(None, "circ", "axial"),
            P(None, None, "circ", "axial"),
            P(None, "circ", "axial"),
            P("circ", "axial"),
            P(None, ("circ", "axial")),
            P(None, None, ("circ", "axial")),
            P(None, ("circ", "axial")),
            P(None, ("circ", "axial")),
            P(("circ", "axial")),
            P(("circ", "axial"), None),
            P(("circ", "axial")),
            P(("circ", "axial")),
            P(None, None, ("circ", "axial")),
            P(None, ("circ", "axial")),
        ),
        out_specs=(P(None, "circ", "axial"), P(None, ("circ", "axial"))),
        check_vma=False,
    )
```
